32 devices in a mesh: grp: 2 (over y), dp: 8 (over z, x), feat: 2 (over core).
Axes of the slice: x: 2, y: 2, z: 4, core: 2. Of those that a mesh axis runs over, the one named last changes fastest.
Arguments:
- node_ids: int32 [2048], P(('grp', 'dp')), parts along dimension 0, may hold values from 0 to 4095, as said below
- hop_table: bfloat16 [8192, 4, 768], P(('grp', 'dp'), None, 'feat'), parts along dimension 0, may hold values from -6 to 6
- w_in: bfloat16 [768, 512], P('feat'), may hold values from -0.21875 to 0.21875
- hop_embed: float32 [4, 512], replicated, may hold values from -5 to 5
- norm_gain: float32 [512], replicated, may hold values from 0.1 to 1.9
- w_qkv: bfloat16 [512, 3, 512], P(None, None, 'feat'), may hold values from -0.25 to 0.25
- w_out: bfloat16 [512, 512], P('feat'), may hold values from -0.25 to 0.25
- cotangent: bfloat16 [2048, 4, 512], P(('grp', 'dp')), parts along dimension 0, may hold values from -0.023925781 to 0.023925781
Outputs:
- grad_in: float32 [1536, 512], P(('grp', 'feat'), 'dp'), parts along dimension 0
- grad_hop: float32 [8, 512], P('grp', 'dp'), parts along dimension 0
- grad_gain: float32 [1024], P(('grp', 'dp')), parts along dimension 0
- grad_qkv: float32 [1024, 3, 512], P(('grp', 'dp'), None, 'feat'), parts along dimension 0
- grad_out: float32 [1024, 512], P(('grp', 'feat'), 'dp'), parts along dimension 0
The draws below stay inside these ranges and needn't reach their ends.
There are 2 independent parts, one for each index of `grp`. The reference program is written for one: setup_inputs(seed, part) draws one part's arguments, and reference() takes and returns one part's arrays. A program takes and returns all parts, laid end to end along the dimension named above; an argument that names none is the same for every part. Nothing has to cross between parts.
Inputs may be any that keep to these rules, and one draw needn't show every extreme that they name: `node_ids`: the ids of one device name exactly 16 rows of each block of 512 consecutive table rows; a row may be named more than once.
All inputs are finite; a program needn't handle non-finite values.
Results may differ from the reference program's by a relative error of at most 0.02.
Values may be sent and summed in bfloat16 or wider, within the bound.
A program may use at most 64 MiB of HBM per device.

```python
import math
import jax
import jax.numpy as jnp
from jax import lax

F = 768
HEADS = 8
HD = 64
D = 512
HOPS = 4
NODE_DEV = 128
TABLE_DEV = 512
NODES = 1024
TABLE = 4096
N_DP = 8
N_FEAT = 2


def draw_node_ids(key, part):
    key = jax.random.fold_in(key, 11)
    key_rows, key_shuffle = jax.random.split(key)
    total = NODE_DEV * N_DP
    position = jnp.arange(total, dtype=jnp.int32)
    owner_of = position % NODE_DEV % N_DP
    local_row = jax.random.randint(key_rows, (total,), 0, TABLE_DEV, dtype=jnp.int32)
    row_ids = (owner_of * TABLE_DEV + local_row).reshape(N_DP, NODE_DEV)
    shuffle_keys = jax.random.split(key_shuffle, N_DP)
    shuffles = jax.vmap(lambda one_key: jax.random.permutation(one_key, NODE_DEV))(shuffle_keys)
    return jnp.take_along_axis(row_ids, shuffles.astype(jnp.int32), axis=1).reshape(total).astype(jnp.int32)


def level_of(stream_key, shape, cuts, smallest, largest):
    gain, own = 1.0, jax.random.fold_in(stream_key, 6)
    for dim, blocks in cuts:
        draws = jnp.exp(jax.random.uniform(jax.random.fold_in(own, dim), (blocks,), jnp.float32, smallest / len(cuts), largest / len(cuts)))
        gain = gain * jnp.repeat(draws, shape[dim] // blocks).reshape([-1 if axis == dim else 1 for axis in range(len(shape))])
    return gain


def scatter_about(own_key, shape, scale, bound, shards=(), kind=jnp.bfloat16):
    entries = jax.random.normal(own_key, shape, jnp.float32) * scale
    if len(shards) > 0:
        entries = level_of(own_key, shape, shards, -0.22, 0.18) * entries
    return jnp.clip(entries, min=-bound, max=bound).astype(kind)


def setup_inputs(seed: int = 0, part: int = 0) -> dict:
    key_list = jax.random.split(jax.random.key(seed), 9)
    part_keys = jax.random.split(jax.random.fold_in(key_list[8], part), 9)
    node_ids = draw_node_ids(jax.random.fold_in(jax.random.fold_in(key_list[8], part), 71), part)
    hop_table = scatter_about(part_keys[1], (TABLE, HOPS, F), 1.0, 6.0, ((0, 8), (2, 2)))
    w_in = scatter_about(key_list[2], (F, D), F ** -0.5, 0.21875, ((0, 2),))
    hop_embed = scatter_about(key_list[3], (HOPS, D), 1.0, 5.0, (), jnp.float32)
    norm_gain = jnp.clip(1.0 + 0.18 * jax.random.normal(key_list[4], (D,), jnp.float32), 0.1, 1.9)
    w_qkv = scatter_about(key_list[5], (D, 3, D), D ** -0.5, 0.25, ((2, 2),))
    w_out = scatter_about(key_list[6], (D, D), D ** -0.5, 0.25, ((0, 2),))
    cotangent = scatter_about(part_keys[7], (NODES, HOPS, D), 0.004, 0.023925781, ((0, 8),))
    return dict(node_ids=node_ids, hop_table=hop_table, w_in=w_in, hop_embed=hop_embed, norm_gain=norm_gain, w_qkv=w_qkv, w_out=w_out, cotangent=cotangent)


EPS = 1e-06

def reference(node_ids, hop_table, w_in, hop_embed, norm_gain, w_qkv, w_out, cotangent):
    f32 = jnp.float32
    bf16 = jnp.bfloat16
    scale = 1.0 / math.sqrt(HD)
    inputs = hop_table[node_ids]
    flat_in = inputs.reshape(NODES * HOPS, F)
    hidden = jnp.dot(flat_in, w_in, preferred_element_type=f32).reshape(NODES, HOPS, D) + hop_embed[None]
    hidden = hidden.reshape(NODES * HOPS, D)
    mean_square = lax.optimization_barrier(jnp.mean(hidden * hidden, axis=-1, keepdims=True))
    inv_root = lax.rsqrt(mean_square + EPS)
    normed = hidden * inv_root
    attn_in = (normed * norm_gain).astype(bf16)
    projected = jnp.dot(attn_in, w_qkv.reshape(D, 3 * D), preferred_element_type=f32).astype(bf16)
    projected = projected.reshape(NODES, HOPS, 3, HEADS, HD)
    query = projected[:, :, 0].astype(f32)
    keys = projected[:, :, 1].astype(f32)
    values = projected[:, :, 2].astype(f32)
    scores = jnp.einsum('nihd,njhd->nhij', query, keys) * scale
    probs = jnp.exp(scores)
    probs = probs / lax.optimization_barrier(jnp.sum(probs, axis=-1, keepdims=True))
    probs_low = probs.astype(bf16).astype(f32)
    mixed = jnp.einsum('nhij,njhd->nihd', probs_low, values).astype(bf16).reshape(NODES * HOPS, D)
    upstream = cotangent.reshape(NODES * HOPS, D)
    grad_out = jnp.dot(mixed.T, upstream, preferred_element_type=f32)
    grad_mixed = jnp.dot(upstream, w_out.T, preferred_element_type=f32).astype(bf16)
    grad_mixed = grad_mixed.astype(f32).reshape(NODES, HOPS, HEADS, HD)
    grad_probs = jnp.einsum('nihd,njhd->nhij', grad_mixed, values)
    grad_values = jnp.einsum('nhij,nihd->njhd', probs_low, grad_mixed)
    grad_scores = probs * (grad_probs - lax.optimization_barrier(jnp.sum(probs * grad_probs, axis=-1, keepdims=True))) * scale
    grad_query = jnp.einsum('nhij,njhd->nihd', grad_scores, keys)
    grad_keys = jnp.einsum('nhij,nihd->njhd', grad_scores, query)
    grad_proj = jnp.stack([grad_query, grad_keys, grad_values], axis=2).astype(bf16)
    grad_proj = grad_proj.reshape(NODES * HOPS, 3, D)
    grad_qkv = jnp.dot(attn_in.T, grad_proj.reshape(NODES * HOPS, 3 * D), preferred_element_type=f32).reshape(D, 3, D)
    width_part = D // N_FEAT
    grad_attn = jnp.zeros((NODES * HOPS, D), f32)
    for feat_part in range(N_FEAT):
        lower = feat_part * width_part
        upper = lower + width_part
        piece = grad_proj[:, :, lower:upper].reshape(NODES * HOPS, 3 * width_part)
        weight_piece = w_qkv[:, :, lower:upper].reshape(D, 3 * width_part)
        partial_sum = jnp.dot(piece, weight_piece.T, preferred_element_type=f32)
        rounded = lax.optimization_barrier(partial_sum.astype(bf16))
        grad_attn = grad_attn + rounded.astype(f32)
    grad_gain = lax.optimization_barrier(jnp.sum(grad_attn * normed, axis=0))
    grad_normed = grad_attn * norm_gain
    grad_hidden = upstream.astype(f32) + inv_root * (grad_normed - normed * lax.optimization_barrier(jnp.mean(grad_normed * normed, axis=-1, keepdims=True)))
    grad_hop = lax.optimization_barrier(jnp.sum(grad_hidden.reshape(NODES, HOPS, D), axis=0))
    grad_in = jnp.dot(flat_in.T, grad_hidden.astype(bf16), preferred_element_type=f32)
    return (grad_in, grad_hop, grad_gain, grad_qkv, grad_out)
```

```python
import functools
import math

import jax
import jax.numpy as jnp
from jax import lax
from jax.experimental import pallas as pl
from jax.experimental.pallas import tpu as pltpu
from jax.sharding import PartitionSpec as P

HD = 64


EPS = 1e-06


def body(node_ids, hop_table, w_in, hop_embed, norm_gain, w_qkv, w_out, cotangent):
    f32 = jnp.float32
    bf16 = jnp.bfloat16
    dp_count = lax.axis_size("dp")
    table_rows = hop_table.shape[0]
    node_count = node_ids.shape[0]
    hop_count = hop_table.shape[1]
    width = w_in.shape[1]
    half_width = w_out.shape[0]
    head_local = half_width // HD
    token_count = node_count * hop_count
    scale = 1.0 / math.sqrt(HD)
    per_owner = node_count // dp_count
    owner_of = node_ids // table_rows
    sort_order = jnp.argsort(owner_of, stable=True)
    asked_rows = (node_ids[sort_order] % table_rows).reshape(dp_count, per_owner)
    found = hop_table[lax.all_to_all(asked_rows, "dp", split_axis=0, concat_axis=0, tiled=True)]
    fetched = lax.all_to_all(found, "dp", split_axis=0, concat_axis=0, tiled=True)
    flat_in = fetched.reshape(token_count, fetched.shape[-1])
    upstream = cotangent[sort_order].reshape(token_count, width)
    full_in, full_weight = (
        lax.all_gather(flat_in, "feat", axis=1, tiled=True),
        lax.all_gather(w_in, "feat", axis=0, tiled=True),
    )
    hidden = jnp.dot(full_in, full_weight, preferred_element_type=f32)
    hidden = (hidden.reshape(node_count, hop_count, width) + hop_embed[None]).reshape(
        token_count, width
    )
    mean_square = jnp.mean(hidden * hidden, axis=-1, keepdims=True)
    inv_root = lax.rsqrt(mean_square + EPS)
    normed = hidden * inv_root
    attn_in = (normed * norm_gain).astype(bf16)
    qkv_weight = w_qkv.reshape(width, 3 * half_width)
    projected = jnp.dot(attn_in, qkv_weight, preferred_element_type=f32).astype(bf16)
    projected = projected.reshape(node_count, hop_count, 3, head_local, HD)
    query = projected[:, :, 0]
    keys = projected[:, :, 1]
    values = projected[:, :, 2]
    scores = jnp.einsum("nihd,njhd->nhij", query, keys, preferred_element_type=f32) * scale
    probs = jnp.exp(scores)
    probs = probs / jnp.sum(probs, axis=-1, keepdims=True)
    probs_low = probs.astype(bf16)
    mixed = jnp.einsum("nhij,njhd->nihd", probs_low, values, preferred_element_type=f32).astype(
        bf16
    )
    mixed = mixed.reshape(token_count, half_width)
    grad_out = jnp.einsum("mc,me->ce", mixed, upstream, preferred_element_type=f32)
    grad_mixed = jnp.einsum("me,ce->mc", upstream, w_out, preferred_element_type=f32).astype(bf16)
    grad_mixed = grad_mixed.reshape(node_count, hop_count, head_local, HD)
    grad_probs = jnp.einsum("nihd,njhd->nhij", grad_mixed, values, preferred_element_type=f32)
    grad_values = jnp.einsum("nhij,nihd->njhd", probs_low, grad_mixed, preferred_element_type=f32)
    grad_scores = probs * (grad_probs - jnp.sum(probs * grad_probs, axis=-1, keepdims=True)) * scale
    grad_query = jnp.einsum("nhij,njhd->nihd", grad_scores, keys.astype(f32))
    grad_keys = jnp.einsum("nhij,nihd->njhd", grad_scores, query.astype(f32))
    grad_proj = jnp.stack([grad_query, grad_keys, grad_values], axis=2).astype(bf16)
    grad_proj = grad_proj.reshape(token_count, 3 * half_width)
    grad_qkv = jnp.einsum("mc,me->ce", attn_in, grad_proj, preferred_element_type=f32).reshape(
        width, 3, half_width
    )
    partial_attn = jnp.einsum(
        "me,ce->mc", grad_proj, qkv_weight, preferred_element_type=f32
    ).astype(bf16)
    grad_attn = lax.psum(partial_attn, "feat").astype(jnp.float32)
    grad_gain = jnp.sum(grad_attn * normed, axis=0)
    grad_normed = grad_attn * norm_gain
    grad_hidden = upstream.astype(f32) + inv_root * (
        grad_normed - normed * jnp.mean(grad_normed * normed, axis=-1, keepdims=True)
    )
    grad_hop = jnp.sum(grad_hidden.reshape(node_count, hop_count, width), axis=0)
    grad_in = jnp.einsum("mc,me->ce", flat_in, grad_hidden.astype(bf16), preferred_element_type=f32)
    summed = (
        lax.psum_scatter(grad_in, "dp", scatter_dimension=1, tiled=True),
        lax.psum_scatter(grad_hop, "dp", scatter_dimension=1, tiled=True),
        lax.psum_scatter(grad_gain, "dp", scatter_dimension=0, tiled=True),
        lax.psum_scatter(grad_qkv, "dp", scatter_dimension=0, tiled=True),
        lax.psum_scatter(grad_out, "dp", scatter_dimension=1, tiled=True),
    )
    return (summed[0], summed[1], summed[2], summed[3], summed[4])


MESH = pl.DeviceIdType.MESH
NT = (((1,), (1,)), ((), ()))
TN = (((0,), (0,)), ((), ()))


def mm(a, b, dims=(((1,), (0,)), ((), ()))):
    return lax.dot_general(a, b, dims, preferred_element_type=jnp.float32)


class Scatter:
    def __init__(self, bits, block, bufs, send_sem, recv_sem, me):
        self.bits, self.block, self.bufs, self.me = bits, block, bufs, me
        self.send_sem, self.recv_sem = send_sem, recv_sem
        self.copies = []

    def bit(self, which):
        return (self.me // (1 << which)) % 2

    def pick(self, stage, side):
        ref = self.block if stage == 0 else self.bufs[2 * stage - 1]
        left = [b for b in (2, 1, 0) if b not in self.bits[:stage]]
        axis = left.index(self.bits[stage])
        index = tuple([slice(None)] * axis + [side])
        return ref.at[index]

    def start(self, stage):
        which = self.bits[stage]
        mine = self.bit(which)
        peer = self.me + (1 - 2 * mine) * (1 << which)
        copy = pltpu.make_async_remote_copy(
            src_ref=self.pick(stage, 1 - mine),
            dst_ref=self.bufs[2 * stage],
            send_sem=self.send_sem.at[stage],
            recv_sem=self.recv_sem.at[stage],
            device_id={"dp": peer},
            device_id_type=MESH,
        )
        copy.start()
        self.copies.append(copy)

    def finish(self, stage):
        self.copies[stage].wait_recv()
        mine = self.bit(self.bits[stage])
        total = self.pick(stage, mine)[...].astype(jnp.float32) + self.bufs[2 * stage][...].astype(
            jnp.float32
        )
        if stage < 2:
            self.bufs[2 * stage + 1][...] = total.astype(jnp.bfloat16)
        return total

    def drain(self):
        for copy in self.copies:
            copy.wait_send()


def kernel(
    dims, ids, tab, w_in, hop_embed, gain, w_qkv, w_out, cot,
    o_qkv, o_out, o_in, o_ext,
    asked, irecv, csend, cot2, xown, xoth, woth, pown, poth, normed_s, proj_s, gm_s, gproj_s, mixed_s,
    vq, q1, q2, q3, q4, q5, vo, o1, o2, o3, o4, o5, vi, i1, i2, i3, i4, i5,
    id_send, id_recv, c_send, c_recv, f_send, f_recv, rs_send, rs_recv,
):
    n, per, hops, table_rows, feat_in, width, half = dims
    f32, bf16 = jnp.float32, jnp.bfloat16
    nodes = n * per
    tokens = nodes * hops
    me = lax.axis_index("dp")
    side = lax.axis_index("feat")

    def peer_of(r):
        return lax.rem(me + r, n)

    barrier = pltpu.get_barrier_semaphore()
    for r in range(1, n):
        pl.semaphore_signal(barrier, inc=1, device_id={"dp": peer_of(r)}, device_id_type=MESH)
    pl.semaphore_signal(barrier, inc=1, device_id={"feat": 1 - side}, device_id_type=MESH)

    ids_f = ids[...].astype(f32)
    owner = jnp.floor((ids_f + 0.5) * (1.0 / table_rows))
    local = ids_f - owner * table_rows
    rows_i = lax.broadcasted_iota(jnp.int32, (nodes, nodes), 0)
    cols_i = lax.broadcasted_iota(jnp.int32, (nodes, nodes), 1)
    wide = jnp.broadcast_to(owner, (nodes, nodes))
    same = jnp.where((wide.T == wide) & (rows_i < cols_i), 1.0, 0.0)
    slot = owner * per + jnp.sum(same, axis=0, keepdims=True)
    place = jnp.where(slot == rows_i.astype(f32), 1.0, 0.0)
    wanted = jnp.sum(place * local, axis=1, keepdims=True)
    asked[...] = jnp.broadcast_to(wanted, (nodes, nodes)).astype(jnp.int32).reshape(n, per, nodes)
    irecv[pl.ds(me, 1)] = asked[pl.ds(me, 1)]

    pl.semaphore_wait(barrier, n)

    def feat_copy(src, dst, k):
        copy = pltpu.make_async_remote_copy(
            src_ref=src, dst_ref=dst, send_sem=f_send.at[k], recv_sem=f_recv.at[k],
            device_id={"feat": 1 - side}, device_id_type=MESH,
        )
        copy.start()
        return copy

    id_copies = []
    for r in range(1, n):
        copy = pltpu.make_async_remote_copy(
            src_ref=asked.at[peer_of(r)], dst_ref=irecv.at[me],
            send_sem=id_send.at[r], recv_sem=id_recv.at[r],
            device_id={"dp": peer_of(r)}, device_id_type=MESH,
        )
        copy.start()
        id_copies.append(copy)
    w_copy = feat_copy(w_in, woth, 0)

    place_low = place.astype(bf16)
    for h in range(hops):
        csend[:, h] = mm(place_low, cot[side, h]).astype(bf16).reshape(n, per, half)
    cot2[side, pl.ds(me, 1)] = csend[pl.ds(me, 1)]
    c_copies = []
    for r in range(1, n):
        copy = pltpu.make_async_remote_copy(
            src_ref=csend.at[peer_of(r)], dst_ref=cot2.at[side, me],
            send_sem=c_send.at[r], recv_sem=c_recv.at[r],
            device_id={"dp": peer_of(r)}, device_id_type=MESH,
        )
        copy.start()
        c_copies.append(copy)

    for copy in id_copies:
        copy.wait_recv()
    got = irecv[...].reshape(nodes, nodes)
    spans = table_rows // nodes
    hot = jnp.concatenate(
        [jnp.where(got == cols_i + nodes * b, 1.0, 0.0).astype(bf16) for b in range(spans)], axis=1
    )
    x_copies = []
    for h in range(hops):
        xown[:, h] = mm(hot, tab[h]).astype(bf16).reshape(n, per, feat_in)
        x_copies.append(feat_copy(xown.at[:, h], xoth.at[:, h], 1 + h))
    x_mine = xown[...].reshape(tokens, feat_in)
    hidden = mm(x_mine, w_in[...])
    w_copy.wait_recv()
    for copy in x_copies:
        copy.wait_recv()
    hidden = hidden + mm(xoth[...].reshape(tokens, feat_in), woth[...])
    hidden = hidden.reshape(n, hops, per, width) + hop_embed[...].reshape(1, hops, 1, width)
    hidden = hidden.reshape(tokens, width)
    inv_root = lax.rsqrt(jnp.mean(hidden * hidden, axis=-1, keepdims=True) + EPS)
    normed = hidden * inv_root
    normed_s[...] = normed
    attn_in = (normed * gain[...]).astype(bf16)
    proj_s[...] = mm(attn_in, w_qkv[...]).astype(bf16).reshape(n, hops, per, 3 * half)

    for copy in c_copies:
        copy.wait_recv()
    cot_copy = feat_copy(cot2.at[side], cot2.at[side], 5)
    cot_copy.wait_recv()
    upstream = jnp.concatenate([cot2[0].reshape(tokens, half), cot2[1].reshape(tokens, half)], axis=1)
    gm_s[...] = mm(upstream, w_out[...], NT).astype(bf16).reshape(n, hops, per, half)

    row_head = lax.broadcasted_iota(jnp.int32, (half, half), 0) // HD
    col_head = lax.broadcasted_iota(jnp.int32, (half, half), 1) // HD
    ones = jnp.where(row_head == col_head, 1.0, 0.0).astype(bf16)
    scale = 1.0 / math.sqrt(HD)
    step = 2
    rows = step * per

    @pl.loop(0, n // step)
    def _(s):
        block = pl.ds(s * step, step)

        def part(ref, i, lo):
            return ref[block, i, :, lo * half : (lo + 1) * half].reshape(rows, half).astype(f32)

        q = [part(proj_s, i, 0) for i in range(hops)]
        k = [part(proj_s, i, 1) for i in range(hops)]
        v = [part(proj_s, i, 2) for i in range(hops)]
        g = [part(gm_s, i, 0) for i in range(hops)]
        grad_k = [0.0] * hops
        grad_v = [0.0] * hops
        for i in range(hops):
            pair = jnp.concatenate([q[i] * k[j] for j in range(hops)], axis=0).astype(bf16)
            e = jnp.exp(mm(pair, ones) * scale)
            e = [e[j * rows : (j + 1) * rows] for j in range(hops)]
            inverse = 1.0 / (e[0] + e[1] + e[2] + e[3])
            p = [t * inverse for t in e]
            low = [t.astype(bf16).astype(f32) for t in p]
            pair = jnp.concatenate([g[i] * v[j] for j in range(hops)], axis=0).astype(bf16)
            gp = mm(pair, ones)
            gp = [gp[j * rows : (j + 1) * rows] for j in range(hops)]
            mixed = sum(low[j] * v[j] for j in range(hops))
            mean = sum(p[j] * gp[j] for j in range(hops))
            gs = [p[j] * (gp[j] - mean) * scale for j in range(hops)]
            grad_q = sum(gs[j] * k[j] for j in range(hops))
            for j in range(hops):
                grad_k[j] = grad_k[j] + gs[j] * q[i]
                grad_v[j] = grad_v[j] + low[j] * g[i]
            mixed_s[block, i] = mixed.astype(bf16).reshape(step, per, half)
            gproj_s[block, i, :, 0:half] = grad_q.astype(bf16).reshape(step, per, half)
        for j in range(hops):
            gproj_s[block, j, :, half : 2 * half] = grad_k[j].astype(bf16).reshape(step, per, half)
            gproj_s[block, j, :, 2 * half :] = grad_v[j].astype(bf16).reshape(step, per, half)

    grad_proj = gproj_s[...].reshape(tokens, 3 * half)
    pown[...] = mm(grad_proj, w_qkv[...], NT).astype(bf16)
    p_copy = feat_copy(pown, poth, 6)

    def scatter(k, bits, block, bufs):
        return Scatter(bits, block, bufs, rs_send.at[k], rs_recv.at[k], me)

    s_qkv = scatter(0, (0, 1, 2), vq, (q1, q2, q3, q4, q5))
    s_out = scatter(1, (1, 0, 2), vo, (o1, o2, o3, o4, o5))
    s_in = scatter(2, (1, 0, 2), vi, (i1, i2, i3, i4, i5))

    vo[...] = mm(upstream, mixed_s[...].reshape(tokens, half), TN).astype(bf16).reshape(vo.shape)
    s_out.start(0)
    vq[...] = mm(attn_in, grad_proj, TN).astype(bf16).reshape(vq.shape)
    s_qkv.start(0)

    p_copy.wait_recv()
    grad_attn = pown[...].astype(f32) + poth[...].astype(f32)
    normed = normed_s[...]
    grad_norm = grad_attn * gain[...]
    grad_hidden = upstream.astype(f32) + inv_root * (
        grad_norm - normed * jnp.mean(grad_norm * normed, axis=-1, keepdims=True)
    )
    grad_low = grad_hidden.astype(bf16)
    gain_low = (grad_attn * normed).astype(bf16)
    lanes = lax.broadcasted_iota(jnp.int32, (tokens, 128), 1)
    hop_of = (lax.broadcasted_iota(jnp.int32, (tokens, 128), 0) // per) % hops
    hop_hot = jnp.where(lanes == hop_of, 1.0, 0.0).astype(bf16)
    gain_hot = jnp.where(lanes == hops, 1.0, 0.0).astype(bf16)
    vi[..., 0:feat_in] = mm(grad_low, x_mine, TN).astype(bf16).reshape(vi.shape[:-1] + (feat_in,))
    ext = mm(grad_low, hop_hot, TN) + mm(gain_low, gain_hot, TN)
    vi[..., feat_in:] = ext.astype(bf16).reshape(vi.shape[:-1] + (128,))
    s_in.start(0)

    all_s = (s_out, s_qkv, s_in)
    for stage in range(2):
        for s in all_s:
            s.finish(stage)
            s.start(stage + 1)
    o_out[...] = s_out.finish(2)
    o_qkv[...] = s_qkv.finish(2)
    last = s_in.finish(2)
    o_in[...] = last[:, 0:feat_in]
    o_ext[...] = last[:, feat_in:]

    for s in all_s:
        s.drain()
    for copy in id_copies + c_copies + x_copies + [w_copy, cot_copy, p_copy]:
        copy.wait_send()


def fused(node_ids, hop_table, w_in, hop_embed, norm_gain, w_qkv, w_out, cotangent):
    f32, bf16 = jnp.float32, jnp.bfloat16
    n = lax.axis_size("dp")
    nodes = node_ids.shape[0]
    per = nodes // n
    table_rows, hops, feat_in = hop_table.shape
    width = w_in.shape[1]
    half = w_out.shape[0]
    tokens = nodes * hops
    share = width // n
    dims = (n, per, hops, table_rows, feat_in, width, half)

    def vm(shape, kind=bf16):
        return pltpu.VMEM(shape, kind)

    def stages(columns):
        c = (share, columns)
        return [vm((2, 2, 2) + c), vm((2, 2) + c), vm((2, 2) + c), vm((2,) + c), vm((2,) + c), vm(c)]

    dma = pltpu.SemaphoreType.DMA
    scratch = [
        vm((n, per, nodes), jnp.int32), vm((n, per, nodes), jnp.int32),
        vm((n, hops, per, half)), vm((2, n, hops, per, half)),
        vm((n, hops, per, feat_in)), vm((n, hops, per, feat_in)), vm((feat_in, width)),
        vm((tokens, width)), vm((tokens, width)), vm((tokens, width), f32),
        vm((n, hops, per, 3 * half)), vm((n, hops, per, half)),
        vm((n, hops, per, 3 * half)), vm((n, hops, per, half)),
    ]
    scratch += stages(3 * half) + stages(half) + stages(feat_in + 128)
    scratch += [dma((n,)), dma((n,)), dma((n,)), dma((n,)), dma((7,)), dma((7,)), dma((3, 3)), dma((3, 3))]
    halves_of = cotangent.reshape(nodes, hops, 2, half).transpose(2, 1, 0, 3)
    vmem = pl.BlockSpec(memory_space=pltpu.VMEM)
    qkv, out, grad_in, ext = pl.pallas_call(
        functools.partial(kernel, dims),
        out_shape=(
            jax.ShapeDtypeStruct((share, 3 * half), f32),
            jax.ShapeDtypeStruct((share, half), f32),
            jax.ShapeDtypeStruct((share, feat_in), f32),
            jax.ShapeDtypeStruct((share, 128), f32),
        ),
        in_specs=[vmem] * 8,
        out_specs=(vmem,) * 4,
        scratch_shapes=scratch,
        compiler_params=pltpu.CompilerParams(
            collective_id=0, has_side_effects=True, vmem_limit_bytes=56 * 1024 * 1024
        ),
    )(
        node_ids.reshape(1, nodes), hop_table.transpose(1, 0, 2), w_in, hop_embed,
        norm_gain.reshape(1, width), w_qkv.reshape(width, 3 * half), w_out, halves_of,
    )
    return (
        grad_in.T, ext[:, 0:hops].T, ext[:, hops], qkv.reshape(share, 3, half), out.T,
    )


def solution(mesh):
    fits = mesh.shape["dp"] == 8 and mesh.shape["feat"] == 2
    placed = (
        P(("grp", "dp")),
        P(("grp", "dp"), None, "feat"),
        P("feat", None),
        P(),
        P(),
        P(None, None, "feat"),
        P("feat", None),
        P(("grp", "dp"), None, None),
    )
    return jax.shard_map(
        fused if fits else body,
        mesh=mesh,
        in_specs=placed,
        out_specs=(
            P(("grp", "feat"), "dp"),
            P("grp", "dp"),
            P(("grp", "dp")),
            P(("grp", "dp"), None, "feat"),
            P(("grp", "feat"), "dp"),
        ),
        check_vma=False,
    )
```

```python
import functools
import math

import jax
import jax.numpy as jnp
from jax import lax
from jax.experimental import pallas as pl
from jax.experimental.pallas import tpu as pltpu
from jax.sharding import PartitionSpec as P

HD = 64


EPS = 1e-06


def body(node_ids, hop_table, w_in, hop_embed, norm_gain, w_qkv, w_out, cotangent):
    f32 = jnp.float32
    bf16 = jnp.bfloat16
    dp_count = lax.axis_size("dp")
    table_rows = hop_table.shape[0]
    node_count = node_ids.shape[0]
    hop_count = hop_table.shape[1]
    width = w_in.shape[1]
    half_width = w_out.shape[0]
    head_local = half_width // HD
    token_count = node_count * hop_count
    scale = 1.0 / math.sqrt(HD)
    per_owner = node_count // dp_count
    owner_of = node_ids // table_rows
    sort_order = jnp.argsort(owner_of, stable=True)
    asked_rows = (node_ids[sort_order] % table_rows).reshape(dp_count, per_owner)
    found = hop_table[lax.all_to_all(asked_rows, "dp", split_axis=0, concat_axis=0, tiled=True)]
    fetched = lax.all_to_all(found, "dp", split_axis=0, concat_axis=0, tiled=True)
    flat_in = fetched.reshape(token_count, fetched.shape[-1])
    upstream = cotangent[sort_order].reshape(token_count, width)
    full_in, full_weight = (
        lax.all_gather(flat_in, "feat", axis=1, tiled=True),
        lax.all_gather(w_in, "feat", axis=0, tiled=True),
    )
    hidden = jnp.dot(full_in, full_weight, preferred_element_type=f32)
    hidden = (hidden.reshape(node_count, hop_count, width) + hop_embed[None]).reshape(
        token_count, width
    )
    mean_square = jnp.mean(hidden * hidden, axis=-1, keepdims=True)
    inv_root = lax.rsqrt(mean_square + EPS)
    normed = hidden * inv_root
    attn_in = (normed * norm_gain).astype(bf16)
    qkv_weight = w_qkv.reshape(width, 3 * half_width)
    projected = jnp.dot(attn_in, qkv_weight, preferred_element_type=f32).astype(bf16)
    projected = projected.reshape(node_count, hop_count, 3, head_local, HD)
    query = projected[:, :, 0]
    keys = projected[:, :, 1]
    values = projected[:, :, 2]
    scores = jnp.einsum("nihd,njhd->nhij", query, keys, preferred_element_type=f32) * scale
    probs = jnp.exp(scores)
    probs = probs / jnp.sum(probs, axis=-1, keepdims=True)
    probs_low = probs.astype(bf16)
    mixed = jnp.einsum("nhij,njhd->nihd", probs_low, values, preferred_element_type=f32).astype(
        bf16
    )
    mixed = mixed.reshape(token_count, half_width)
    grad_out = jnp.einsum("mc,me->ce", mixed, upstream, preferred_element_type=f32)
    grad_mixed = jnp.einsum("me,ce->mc", upstream, w_out, preferred_element_type=f32).astype(bf16)
    grad_mixed = grad_mixed.reshape(node_count, hop_count, head_local, HD)
    grad_probs = jnp.einsum("nihd,njhd->nhij", grad_mixed, values, preferred_element_type=f32)
    grad_values = jnp.einsum("nhij,nihd->njhd", probs_low, grad_mixed, preferred_element_type=f32)
    grad_scores = probs * (grad_probs - jnp.sum(probs * grad_probs, axis=-1, keepdims=True)) * scale
    grad_query = jnp.einsum("nhij,njhd->nihd", grad_scores, keys.astype(f32))
    grad_keys = jnp.einsum("nhij,nihd->njhd", grad_scores, query.astype(f32))
    grad_proj = jnp.stack([grad_query, grad_keys, grad_values], axis=2).astype(bf16)
    grad_proj = grad_proj.reshape(token_count, 3 * half_width)
    grad_qkv = jnp.einsum("mc,me->ce", attn_in, grad_proj, preferred_element_type=f32).reshape(
        width, 3, half_width
    )
    partial_attn = jnp.einsum(
        "me,ce->mc", grad_proj, qkv_weight, preferred_element_type=f32
    ).astype(bf16)
    grad_attn = lax.psum(partial_attn, "feat").astype(jnp.float32)
    grad_gain = jnp.sum(grad_attn * normed, axis=0)
    grad_normed = grad_attn * norm_gain
    grad_hidden = upstream.astype(f32) + inv_root * (
        grad_normed - normed * jnp.mean(grad_normed * normed, axis=-1, keepdims=True)
    )
    grad_hop = jnp.sum(grad_hidden.reshape(node_count, hop_count, width), axis=0)
    grad_in = jnp.einsum("mc,me->ce", flat_in, grad_hidden.astype(bf16), preferred_element_type=f32)
    summed = (
        lax.psum_scatter(grad_in, "dp", scatter_dimension=1, tiled=True),
        lax.psum_scatter(grad_hop, "dp", scatter_dimension=1, tiled=True),
        lax.psum_scatter(grad_gain, "dp", scatter_dimension=0, tiled=True),
        lax.psum_scatter(grad_qkv, "dp", scatter_dimension=0, tiled=True),
        lax.psum_scatter(grad_out, "dp", scatter_dimension=1, tiled=True),
    )
    return (summed[0], summed[1], summed[2], summed[3], summed[4])


MESH = pl.DeviceIdType.MESH
NT = (((1,), (1,)), ((), ()))
TN = (((0,), (0,)), ((), ()))


def mm(a, b, dims=(((1,), (0,)), ((), ()))):
    return lax.dot_general(a, b, dims, preferred_element_type=jnp.float32)


class Scatter:
    def __init__(self, bits, block, bufs, send_sem, recv_sem, me):
        self.bits, self.block, self.bufs, self.me = bits, block, bufs, me
        self.send_sem, self.recv_sem = send_sem, recv_sem
        self.copies = []

    def bit(self, which):
        return (self.me // (1 << which)) % 2

    def pick(self, stage, side):
        ref = self.block if stage == 0 else self.bufs[2 * stage - 1]
        left = [b for b in (2, 1, 0) if b not in self.bits[:stage]]
        axis = left.index(self.bits[stage])
        index = tuple([slice(None)] * axis + [side])
        return ref.at[index]

    def start(self, stage):
        which = self.bits[stage]
        mine = self.bit(which)
        peer = self.me + (1 - 2 * mine) * (1 << which)
        copy = pltpu.make_async_remote_copy(
            src_ref=self.pick(stage, 1 - mine),
            dst_ref=self.bufs[2 * stage],
            send_sem=self.send_sem.at[stage],
            recv_sem=self.recv_sem.at[stage],
            device_id={"dp": peer},
            device_id_type=MESH,
        )
        copy.start()
        self.copies.append(copy)

    def finish(self, stage):
        self.copies[stage].wait_recv()
        mine = self.bit(self.bits[stage])
        total = self.pick(stage, mine)[...].astype(jnp.float32) + self.bufs[2 * stage][...].astype(
            jnp.float32
        )
        if stage < 2:
            self.bufs[2 * stage + 1][...] = total.astype(jnp.bfloat16)
        return total

    def drain(self):
        for copy in self.copies:
            copy.wait_send()


def kernel(
    dims, ids, tab_hbm, w_in_hbm, hop_embed, gain, w_qkv_hbm, w_out_hbm, cot_hbm,
    o0, o1, o2, o3,
    tab_in, w_in, w_qkv, w_out, cot_in, tab, cot,
    asked, irecv, csend, cot2, xown, xoth, woth, pown, poth, normed_s, proj_s, gm_s, gproj_s, mixed_s,
    a0, a1, a2, a3, a4, a5, b0, b1, b2, b3, b4, b5, c0, c1, c2, c3, c4, c5, d0, d1, d2, d3, d4, d5,
    in_sem, id_send, id_recv, c_send, c_recv, f_send, f_recv, rs_send, rs_recv,
):
    n, per, hops, table_rows, feat_in, width, half = dims
    f32, bf16 = jnp.float32, jnp.bfloat16
    nodes = n * per
    tokens = nodes * hops
    me = lax.axis_index("dp")
    side = lax.axis_index("feat")

    def peer_of(r):
        return lax.rem(me + r, n)

    loads = []

    def load(src, dst):
        copy = pltpu.make_async_copy(src, dst, in_sem.at[len(loads)])
        copy.start()
        loads.append(copy)
        return copy

    cot_load = load(cot_hbm, cot_in)
    tab_load = load(tab_hbm, tab_in)
    w_in_load = load(w_in_hbm, w_in)
    w_qkv_loads = [
        load(w_qkv_hbm.at[c], w_qkv.at[:, c * half : (c + 1) * half]) for c in range(3)
    ]
    w_out_load = load(w_out_hbm, w_out)

    barrier = pltpu.get_barrier_semaphore()
    for r in range(1, n):
        pl.semaphore_signal(barrier, inc=1, device_id={"dp": peer_of(r)}, device_id_type=MESH)
    pl.semaphore_signal(barrier, inc=1, device_id={"feat": 1 - side}, device_id_type=MESH)

    ids_f = ids[...].astype(f32)
    owner = jnp.floor((ids_f + 0.5) * (1.0 / table_rows))
    local = ids_f - owner * table_rows
    rows_i = lax.broadcasted_iota(jnp.int32, (nodes, nodes), 0)
    cols_i = lax.broadcasted_iota(jnp.int32, (nodes, nodes), 1)
    wide = jnp.broadcast_to(owner, (nodes, nodes))
    same = jnp.where((wide.T == wide) & (rows_i < cols_i), 1.0, 0.0)
    slot = owner * per + jnp.sum(same, axis=0, keepdims=True)
    place = jnp.where(slot == rows_i.astype(f32), 1.0, 0.0)
    wanted = jnp.sum(place * local, axis=1, keepdims=True)
    asked[...] = jnp.broadcast_to(wanted, (nodes, nodes)).astype(jnp.int32).reshape(n, per, nodes)
    irecv[pl.ds(me, 1)] = asked[pl.ds(me, 1)]

    pl.semaphore_wait(barrier, n)

    def feat_copy(src, dst, k):
        copy = pltpu.make_async_remote_copy(
            src_ref=src, dst_ref=dst, send_sem=f_send.at[k], recv_sem=f_recv.at[k],
            device_id={"feat": 1 - side}, device_id_type=MESH,
        )
        copy.start()
        return copy

    id_copies = []
    for r in range(1, n):
        copy = pltpu.make_async_remote_copy(
            src_ref=asked.at[peer_of(r)], dst_ref=irecv.at[me],
            send_sem=id_send.at[r], recv_sem=id_recv.at[r],
            device_id={"dp": peer_of(r)}, device_id_type=MESH,
        )
        copy.start()
        id_copies.append(copy)
    w_copy = feat_copy(w_in_hbm, woth, 0)
    cot_load.wait()
    cot[...] = jnp.swapaxes(cot_in[...], 0, 1)

    place_low = place.astype(bf16)
    for h in range(hops):
        csend[:, h] = mm(place_low, cot[h, :, pl.ds(pl.multiple_of(side * half, half), half)]).astype(bf16).reshape(n, per, half)
    cot2[side, pl.ds(me, 1)] = csend[pl.ds(me, 1)]
    c_copies = []
    for r in range(1, n):
        copy = pltpu.make_async_remote_copy(
            src_ref=csend.at[peer_of(r)], dst_ref=cot2.at[side, me],
            send_sem=c_send.at[r], recv_sem=c_recv.at[r],
            device_id={"dp": peer_of(r)}, device_id_type=MESH,
        )
        copy.start()
        c_copies.append(copy)

    tab_load.wait()
    tab[...] = jnp.swapaxes(tab_in[...], 0, 1)
    for copy in id_copies:
        copy.wait_recv()
    got = irecv[...].reshape(nodes, nodes)
    spans = table_rows // nodes
    hot = jnp.concatenate(
        [jnp.where(got == cols_i + nodes * b, 1.0, 0.0).astype(bf16) for b in range(spans)], axis=1
    )
    x_copies = []
    for h in range(hops):
        xown[:, h] = mm(hot, tab[h]).astype(bf16).reshape(n, per, feat_in)
        x_copies.append(feat_copy(xown.at[:, h], xoth.at[:, h], 1 + h))
    x_mine = xown[...].reshape(tokens, feat_in)
    w_in_load.wait()
    hidden = mm(x_mine, w_in[...])
    w_copy.wait_recv()
    for copy in x_copies:
        copy.wait_recv()
    hidden = hidden + mm(xoth[...].reshape(tokens, feat_in), woth[...])
    hidden = hidden.reshape(n, hops, per, width) + hop_embed[...].reshape(1, hops, 1, width)
    hidden = hidden.reshape(tokens, width)
    inv_root = lax.rsqrt(jnp.mean(hidden * hidden, axis=-1, keepdims=True) + EPS)
    normed = hidden * inv_root
    normed_s[...] = normed
    attn_in = (normed * gain[...]).astype(bf16)
    for copy in w_qkv_loads:
        copy.wait()
    proj_s[...] = mm(attn_in, w_qkv[...]).astype(bf16).reshape(n, hops, per, 3 * half)

    for copy in c_copies:
        copy.wait_recv()
    cot_copy = feat_copy(cot2.at[side], cot2.at[side], 5)
    cot_copy.wait_recv()
    upstream = jnp.concatenate([cot2[0].reshape(tokens, half), cot2[1].reshape(tokens, half)], axis=1)
    w_out_load.wait()
    gm_s[...] = mm(upstream, w_out[...], NT).astype(bf16).reshape(n, hops, per, half)

    row_head = lax.broadcasted_iota(jnp.int32, (half, half), 0) // HD
    col_head = lax.broadcasted_iota(jnp.int32, (half, half), 1) // HD
    ones = jnp.where(row_head == col_head, 1.0, 0.0).astype(bf16)
    scale = 1.0 / math.sqrt(HD)
    step = 2
    rows = step * per

    @pl.loop(0, n // step)
    def _(s):
        block = pl.ds(s * step, step)

        def part(ref, i, lo):
            return ref[block, i, :, lo * half : (lo + 1) * half].reshape(rows, half).astype(f32)

        q = [part(proj_s, i, 0) for i in range(hops)]
        k = [part(proj_s, i, 1) for i in range(hops)]
        v = [part(proj_s, i, 2) for i in range(hops)]
        g = [part(gm_s, i, 0) for i in range(hops)]
        grad_k = [0.0] * hops
        grad_v = [0.0] * hops
        for i in range(hops):
            pair = jnp.concatenate([q[i] * k[j] for j in range(hops)], axis=0).astype(bf16)
            e = jnp.exp(mm(pair, ones) * scale)
            e = [e[j * rows : (j + 1) * rows] for j in range(hops)]
            inverse = 1.0 / (e[0] + e[1] + e[2] + e[3])
            p = [t * inverse for t in e]
            low = [t.astype(bf16).astype(f32) for t in p]
            pair = jnp.concatenate([g[i] * v[j] for j in range(hops)], axis=0).astype(bf16)
            gp = mm(pair, ones)
            gp = [gp[j * rows : (j + 1) * rows] for j in range(hops)]
            mixed = sum(low[j] * v[j] for j in range(hops))
            mean = sum(p[j] * gp[j] for j in range(hops))
            gs = [p[j] * (gp[j] - mean) * scale for j in range(hops)]
            grad_q = sum(gs[j] * k[j] for j in range(hops))
            for j in range(hops):
                grad_k[j] = grad_k[j] + gs[j] * q[i]
                grad_v[j] = grad_v[j] + low[j] * g[i]
            mixed_s[block, i] = mixed.astype(bf16).reshape(step, per, half)
            gproj_s[block, i, :, 0:half] = grad_q.astype(bf16).reshape(step, per, half)
        for j in range(hops):
            gproj_s[block, j, :, half : 2 * half] = grad_k[j].astype(bf16).reshape(step, per, half)
            gproj_s[block, j, :, 2 * half :] = grad_v[j].astype(bf16).reshape(step, per, half)

    grad_proj = gproj_s[...].reshape(tokens, 3 * half)
    pown[...] = mm(grad_proj, w_qkv[...], NT).astype(bf16)
    p_copy = feat_copy(pown, poth, 6)

    def scatter(k, bits, block, bufs):
        return Scatter(bits, block, bufs, rs_send.at[k], rs_recv.at[k], me)

    s0 = scatter(0, (0, 1, 2), a0, (a1, a2, a3, a4, a5))
    s1 = scatter(1, (1, 0, 2), b0, (b1, b2, b3, b4, b5))
    s2 = scatter(2, (0, 1, 2), c0, (c1, c2, c3, c4, c5))
    s3 = scatter(3, (1, 0, 2), d0, (d1, d2, d3, d4, d5))

    def put(ref, lo, value):
        ref[..., lo : lo + value.shape[1]] = value.astype(bf16).reshape(
            ref.shape[:-1] + (value.shape[1],)
        )

    put(b0, 0, mm(attn_in, grad_proj[:, 2 * half :], TN))
    put(b0, half, mm(upstream, mixed_s[...].reshape(tokens, half), TN))
    s1.start(0)
    put(a0, 0, mm(attn_in, grad_proj[:, 0 : 2 * half], TN))
    s0.start(0)

    p_copy.wait_recv()
    grad_attn = pown[...].astype(f32) + poth[...].astype(f32)
    normed = normed_s[...]
    grad_norm = grad_attn * gain[...]
    grad_hidden = upstream.astype(f32) + inv_root * (
        grad_norm - normed * jnp.mean(grad_norm * normed, axis=-1, keepdims=True)
    )
    grad_low = grad_hidden.astype(bf16)
    gain_low = (grad_attn * normed).astype(bf16)
    lanes = lax.broadcasted_iota(jnp.int32, (tokens, 128), 1)
    hop_of = (lax.broadcasted_iota(jnp.int32, (tokens, 128), 0) // per) % hops
    hop_hot = jnp.where(lanes == hop_of, 1.0, 0.0).astype(bf16)
    gain_hot = jnp.where(lanes == hops, 1.0, 0.0).astype(bf16)
    rest = feat_in - 128
    put(d0, 0, mm(grad_low, x_mine[:, rest:], TN))
    put(d0, 128, mm(grad_low, hop_hot, TN) + mm(gain_low, gain_hot, TN))
    s3.start(0)
    put(c0, 0, mm(grad_low, x_mine[:, 0:rest], TN))
    s2.start(0)

    all_s = (s1, s0, s3, s2)
    for stage in range(2):
        for s in all_s:
            s.finish(stage)
            s.start(stage + 1)
    o1[...] = s1.finish(2)
    o0[...] = s0.finish(2)
    o3[...] = s3.finish(2)
    o2[...] = s2.finish(2)
    for s in all_s:
        s.drain()
    for copy in id_copies + c_copies + x_copies + [w_copy, cot_copy, p_copy]:
        copy.wait_send()


def lay_out(hops, half, feat_in, b0, b1, b2, b3, qkv, out, grad_in, grad_hop, grad_gain):
    rest = feat_in - 128
    qkv[0] = b0[:, 0:half]
    qkv[1] = b0[:, half:]
    qkv[2] = b1[:, 0:half]
    out[...] = b1[:, half:]
    grad_in[:, 0:rest] = b2[...]
    grad_in[:, rest:] = b3[:, 0:128]
    turned = b3[:, 128:].T
    grad_hop[...] = turned[0:hops]
    grad_gain[...] = turned[hops : hops + 1]


def fused(node_ids, hop_table, w_in, hop_embed, norm_gain, w_qkv, w_out, cotangent):
    f32, bf16 = jnp.float32, jnp.bfloat16
    n = lax.axis_size("dp")
    nodes = node_ids.shape[0]
    per = nodes // n
    table_rows, hops, feat_in = hop_table.shape
    width = w_in.shape[1]
    half = w_out.shape[0]
    tokens = nodes * hops
    share = width // n
    dims = (n, per, hops, table_rows, feat_in, width, half)

    def vm(shape, kind=bf16):
        return pltpu.VMEM(shape, kind)

    def stages(columns):
        c = (share, columns)
        return [vm((2, 2, 2) + c), vm((2, 2) + c), vm((2, 2) + c), vm((2,) + c), vm((2,) + c), vm(c)]

    dma = pltpu.SemaphoreType.DMA
    scratch = [
        vm((table_rows, hops, feat_in)), vm((feat_in, width)), vm((width, 3 * half)), vm((half, width)),
        vm((nodes, hops, width)), vm((hops, table_rows, feat_in)), vm((hops, nodes, width)),
        vm((n, per, nodes), jnp.int32), vm((n, per, nodes), jnp.int32),
        vm((n, hops, per, half)), vm((2, n, hops, per, half)),
        vm((n, hops, per, feat_in)), vm((n, hops, per, feat_in)), vm((feat_in, width)),
        vm((tokens, width)), vm((tokens, width)), vm((tokens, width), f32),
        vm((n, hops, per, 3 * half)), vm((n, hops, per, half)),
        vm((n, hops, per, 3 * half)), vm((n, hops, per, half)),
    ]
    scratch += stages(2 * half) + stages(2 * half) + stages(feat_in - 128) + stages(256)
    scratch += [dma((7,)), dma((n,)), dma((n,)), dma((n,)), dma((n,)), dma((7,)), dma((7,)), dma((4, 3)), dma((4, 3))]
    vmem = pl.BlockSpec(memory_space=pltpu.VMEM)
    hbm = pl.BlockSpec(memory_space=pl.ANY)
    blocks = pl.pallas_call(
        functools.partial(kernel, dims),
        out_shape=tuple(
            jax.ShapeDtypeStruct((share, c), f32) for c in (2 * half, 2 * half, feat_in - 128, 256)
        ),
        in_specs=[vmem, hbm, hbm, vmem, vmem, hbm, hbm, hbm],
        out_specs=(vmem,) * 4,
        scratch_shapes=scratch,
        compiler_params=pltpu.CompilerParams(
            collective_id=0, has_side_effects=True, vmem_limit_bytes=56 * 1024 * 1024
        ),
    )(
        node_ids.reshape(1, nodes), hop_table, w_in, hop_embed,
        norm_gain.reshape(1, width), w_qkv.transpose(1, 0, 2), w_out, cotangent,
    )
    qkv, out, grad_in, grad_hop, grad_gain = pl.pallas_call(
        functools.partial(lay_out, hops, half, feat_in),
        out_shape=(
            jax.ShapeDtypeStruct((3, share, half), f32),
            jax.ShapeDtypeStruct((share, half), f32),
            jax.ShapeDtypeStruct((share, feat_in), f32),
            jax.ShapeDtypeStruct((hops, share), f32),
            jax.ShapeDtypeStruct((1, share), f32),
        ),
        in_specs=[vmem] * 4,
        out_specs=(vmem,) * 5,
    )(*blocks)
    return grad_in.T, grad_hop, grad_gain.reshape(share), qkv.transpose(1, 0, 2), out.T


def solution(mesh):
    fits = mesh.shape["dp"] == 8 and mesh.shape["feat"] == 2
    placed = (
        P(("grp", "dp")),
        P(("grp", "dp"), None, "feat"),
        P("feat", None),
        P(),
        P(),
        P(None, None, "feat"),
        P("feat", None),
        P(("grp", "dp"), None, None),
    )
    return jax.shard_map(
        fused if fits else body,
        mesh=mesh,
        in_specs=placed,
        out_specs=(
            P(("grp", "feat"), "dp"),
            P("grp", "dp"),
            P(("grp", "dp")),
            P(("grp", "dp"), None, "feat"),
            P(("grp", "feat"), "dp"),
        ),
        check_vma=False,
    )
```

```python
import functools
import math

import jax
import jax.numpy as jnp
from jax import lax
from jax.experimental import pallas as pl
from jax.experimental.pallas import tpu as pltpu
from jax.sharding import PartitionSpec as P

HD = 64


EPS = 1e-06


def body(node_ids, hop_table, w_in, hop_embed, norm_gain, w_qkv, w_out, cotangent):
    f32 = jnp.float32
    bf16 = jnp.bfloat16
    dp_count = lax.axis_size("dp")
    table_rows = hop_table.shape[0]
    node_count = node_ids.shape[0]
    hop_count = hop_table.shape[1]
    width = w_in.shape[1]
    half_width = w_out.shape[0]
    head_local = half_width // HD
    token_count = node_count * hop_count
    scale = 1.0 / math.sqrt(HD)
    per_owner = node_count // dp_count
    owner_of = node_ids // table_rows
    sort_order = jnp.argsort(owner_of, stable=True)
    asked_rows = (node_ids[sort_order] % table_rows).reshape(dp_count, per_owner)
    found = hop_table[lax.all_to_all(asked_rows, "dp", split_axis=0, concat_axis=0, tiled=True)]
    fetched = lax.all_to_all(found, "dp", split_axis=0, concat_axis=0, tiled=True)
    flat_in = fetched.reshape(token_count, fetched.shape[-1])
    upstream = cotangent[sort_order].reshape(token_count, width)
    full_in, full_weight = (
        lax.all_gather(flat_in, "feat", axis=1, tiled=True),
        lax.all_gather(w_in, "feat", axis=0, tiled=True),
    )
    hidden = jnp.dot(full_in, full_weight, preferred_element_type=f32)
    hidden = (hidden.reshape(node_count, hop_count, width) + hop_embed[None]).reshape(
        token_count, width
    )
    mean_square = jnp.mean(hidden * hidden, axis=-1, keepdims=True)
    inv_root = lax.rsqrt(mean_square + EPS)
    normed = hidden * inv_root
    attn_in = (normed * norm_gain).astype(bf16)
    qkv_weight = w_qkv.reshape(width, 3 * half_width)
    projected = jnp.dot(attn_in, qkv_weight, preferred_element_type=f32).astype(bf16)
    projected = projected.reshape(node_count, hop_count, 3, head_local, HD)
    query = projected[:, :, 0]
    keys = projected[:, :, 1]
    values = projected[:, :, 2]
    scores = jnp.einsum("nihd,njhd->nhij", query, keys, preferred_element_type=f32) * scale
    probs = jnp.exp(scores)
    probs = probs / jnp.sum(probs, axis=-1, keepdims=True)
    probs_low = probs.astype(bf16)
    mixed = jnp.einsum("nhij,njhd->nihd", probs_low, values, preferred_element_type=f32).astype(
        bf16
    )
    mixed = mixed.reshape(token_count, half_width)
    grad_out = jnp.einsum("mc,me->ce", mixed, upstream, preferred_element_type=f32)
    grad_mixed = jnp.einsum("me,ce->mc", upstream, w_out, preferred_element_type=f32).astype(bf16)
    grad_mixed = grad_mixed.reshape(node_count, hop_count, head_local, HD)
    grad_probs = jnp.einsum("nihd,njhd->nhij", grad_mixed, values, preferred_element_type=f32)
    grad_values = jnp.einsum("nhij,nihd->njhd", probs_low, grad_mixed, preferred_element_type=f32)
    grad_scores = probs * (grad_probs - jnp.sum(probs * grad_probs, axis=-1, keepdims=True)) * scale
    grad_query = jnp.einsum("nhij,njhd->nihd", grad_scores, keys.astype(f32))
    grad_keys = jnp.einsum("nhij,nihd->njhd", grad_scores, query.astype(f32))
    grad_proj = jnp.stack([grad_query, grad_keys, grad_values], axis=2).astype(bf16)
    grad_proj = grad_proj.reshape(token_count, 3 * half_width)
    grad_qkv = jnp.einsum("mc,me->ce", attn_in, grad_proj, preferred_element_type=f32).reshape(
        width, 3, half_width
    )
    partial_attn = jnp.einsum(
        "me,ce->mc", grad_proj, qkv_weight, preferred_element_type=f32
    ).astype(bf16)
    grad_attn = lax.psum(partial_attn, "feat").astype(jnp.float32)
    grad_gain = jnp.sum(grad_attn * normed, axis=0)
    grad_normed = grad_attn * norm_gain
    grad_hidden = upstream.astype(f32) + inv_root * (
        grad_normed - normed * jnp.mean(grad_normed * normed, axis=-1, keepdims=True)
    )
    grad_hop = jnp.sum(grad_hidden.reshape(node_count, hop_count, width), axis=0)
    grad_in = jnp.einsum("mc,me->ce", flat_in, grad_hidden.astype(bf16), preferred_element_type=f32)
    summed = (
        lax.psum_scatter(grad_in, "dp", scatter_dimension=1, tiled=True),
        lax.psum_scatter(grad_hop, "dp", scatter_dimension=1, tiled=True),
        lax.psum_scatter(grad_gain, "dp", scatter_dimension=0, tiled=True),
        lax.psum_scatter(grad_qkv, "dp", scatter_dimension=0, tiled=True),
        lax.psum_scatter(grad_out, "dp", scatter_dimension=1, tiled=True),
    )
    return (summed[0], summed[1], summed[2], summed[3], summed[4])


MESH = pl.DeviceIdType.MESH
NT = (((1,), (1,)), ((), ()))
TN = (((0,), (0,)), ((), ()))


def mm(a, b, dims=(((1,), (0,)), ((), ()))):
    return lax.dot_general(a, b, dims, preferred_element_type=jnp.float32)


class Scatter:
    def __init__(self, bits, block, bufs, send_sem, recv_sem, me):
        self.bits, self.block, self.bufs, self.me = bits, block, bufs, me
        self.send_sem, self.recv_sem = send_sem, recv_sem
        self.copies = []

    def bit(self, which):
        return (self.me // (1 << which)) % 2

    def pick(self, stage, side):
        ref = self.block if stage == 0 else self.bufs[2 * stage - 1]
        left = [b for b in (2, 1, 0) if b not in self.bits[:stage]]
        axis = left.index(self.bits[stage])
        index = tuple([slice(None)] * axis + [side])
        return ref.at[index]

    def start(self, stage):
        which = self.bits[stage]
        mine = self.bit(which)
        peer = self.me + (1 - 2 * mine) * (1 << which)
        copy = pltpu.make_async_remote_copy(
            src_ref=self.pick(stage, 1 - mine),
            dst_ref=self.bufs[2 * stage],
            send_sem=self.send_sem.at[stage],
            recv_sem=self.recv_sem.at[stage],
            device_id={"dp": peer},
            device_id_type=MESH,
        )
        copy.start()
        self.copies.append(copy)

    def finish(self, stage):
        self.copies[stage].wait_recv()
        mine = self.bit(self.bits[stage])
        total = self.pick(stage, mine)[...].astype(jnp.float32) + self.bufs[2 * stage][...].astype(
            jnp.float32
        )
        if stage < 2:
            self.bufs[2 * stage + 1][...] = total.astype(jnp.bfloat16)
        return total

    def drain(self):
        for copy in self.copies:
            copy.wait_send()


class DirectScatter(Scatter):
    def block_of(self, r):
        high, low = self.bit(2), self.bit(1)
        return (1 - high if r & 2 else high), (1 - low if r & 1 else low)

    def start(self, stage):
        if stage == 0:
            super().start(0)
        if stage != 1:
            return
        for r in (1, 2, 3):
            high, low = self.block_of(r)
            copy = pltpu.make_async_remote_copy(
                src_ref=self.bufs[1].at[high, low],
                dst_ref=self.bufs[4] if r == 3 else self.bufs[2].at[r - 1],
                send_sem=self.send_sem.at[r],
                recv_sem=self.recv_sem.at[r],
                device_id={"dp": 4 * high + 2 * low + self.bit(0)},
                device_id_type=MESH,
            )
            copy.start()
            self.copies.append(copy)

    def finish(self, stage):
        if stage == 0:
            return super().finish(0)
        if stage == 1:
            return None
        for copy in self.copies[1:]:
            copy.wait_recv()
        high, low = self.block_of(0)
        total = self.bufs[1][high, low].astype(jnp.float32)
        for part in (self.bufs[2][0], self.bufs[2][1], self.bufs[4][...]):
            total = total + part.astype(jnp.float32)
        return total


def kernel(
    dims, ids, tab_hbm, w_in_hbm, hop_embed, gain, w_qkv_hbm, w_out_hbm, cot_hbm,
    o_q, o_k, o_v, o_out, o_in, o_ext,
    tab_in, w_in, w_qkv, w_out, cot_in, tab, cot,
    asked, irecv, csend, cot2, xown, xoth, woth, pown, poth, normed_s, proj_s, gm_s, gproj_s, mixed_s,
    p_s, *rest,
):
    n, per, hops, table_rows, feat_in, width, half = dims
    in_sem, id_send, id_recv, c_send, c_recv, f_send, f_recv, rs_send, rs_recv = rest[36:]
    f32, bf16 = jnp.float32, jnp.bfloat16
    nodes = n * per
    tokens = nodes * hops
    me = lax.axis_index("dp")
    side = lax.axis_index("feat")

    def peer_of(r):
        return lax.rem(me + r, n)

    loads = []

    def load(src, dst):
        copy = pltpu.make_async_copy(src, dst, in_sem.at[len(loads)])
        copy.start()
        loads.append(copy)
        return copy

    cot_load = load(cot_hbm, cot_in)
    tab_load = load(tab_hbm, tab_in)
    w_in_load = load(w_in_hbm, w_in)
    w_qkv_loads = [
        load(w_qkv_hbm.at[c], w_qkv.at[:, c * half : (c + 1) * half]) for c in range(3)
    ]
    w_out_load = load(w_out_hbm, w_out)

    barrier = pltpu.get_barrier_semaphore()
    for r in range(1, n):
        pl.semaphore_signal(barrier, inc=1, device_id={"dp": peer_of(r)}, device_id_type=MESH)
    pl.semaphore_signal(barrier, inc=1, device_id={"feat": 1 - side}, device_id_type=MESH)

    ids_f = ids[...].astype(f32)
    owner = jnp.floor((ids_f + 0.5) * (1.0 / table_rows))
    local = ids_f - owner * table_rows
    rows_i = lax.broadcasted_iota(jnp.int32, (nodes, nodes), 0)
    cols_i = lax.broadcasted_iota(jnp.int32, (nodes, nodes), 1)
    wide = jnp.broadcast_to(owner, (nodes, nodes))
    same = jnp.where((wide.T == wide) & (rows_i < cols_i), 1.0, 0.0)
    slot = owner * per + jnp.sum(same, axis=0, keepdims=True)
    place = jnp.where(slot == rows_i.astype(f32), 1.0, 0.0)
    wanted = jnp.sum(place * local, axis=1, keepdims=True)
    asked[...] = jnp.broadcast_to(wanted, (nodes, nodes)).astype(jnp.int32).reshape(n, per, nodes)
    irecv[pl.ds(me, 1)] = asked[pl.ds(me, 1)]

    pl.semaphore_wait(barrier, n)

    def feat_copy(src, dst, k):
        copy = pltpu.make_async_remote_copy(
            src_ref=src, dst_ref=dst, send_sem=f_send.at[k], recv_sem=f_recv.at[k],
            device_id={"feat": 1 - side}, device_id_type=MESH,
        )
        copy.start()
        return copy

    id_copies = []
    for r in range(1, n):
        copy = pltpu.make_async_remote_copy(
            src_ref=asked.at[peer_of(r)], dst_ref=irecv.at[me],
            send_sem=id_send.at[r], recv_sem=id_recv.at[r],
            device_id={"dp": peer_of(r)}, device_id_type=MESH,
        )
        copy.start()
        id_copies.append(copy)
    w_copy = feat_copy(w_in_hbm, woth, 0)
    cot_load.wait()
    cot[...] = jnp.swapaxes(cot_in[...], 0, 1)

    place_low = place.astype(bf16)
    for h in range(hops):
        csend[:, h] = mm(place_low, cot[h, :, pl.ds(pl.multiple_of(side * half, half), half)]).astype(bf16).reshape(n, per, half)
    cot2[side, pl.ds(me, 1)] = csend[pl.ds(me, 1)]
    c_copies = []
    for r in range(1, n):
        copy = pltpu.make_async_remote_copy(
            src_ref=csend.at[peer_of(r)], dst_ref=cot2.at[side, me],
            send_sem=c_send.at[r], recv_sem=c_recv.at[r],
            device_id={"dp": peer_of(r)}, device_id_type=MESH,
        )
        copy.start()
        c_copies.append(copy)

    tab_load.wait()
    tab[...] = jnp.swapaxes(tab_in[...], 0, 1)
    for copy in id_copies:
        copy.wait_recv()
    got = irecv[...].reshape(nodes, nodes)
    spans = table_rows // nodes
    hot = jnp.concatenate(
        [jnp.where(got == cols_i + nodes * b, 1.0, 0.0).astype(bf16) for b in range(spans)], axis=1
    )
    x_copies = []
    for h in range(hops):
        xown[:, h] = mm(hot, tab[h]).astype(bf16).reshape(n, per, feat_in)
        x_copies.append(feat_copy(xown.at[:, h], xoth.at[:, h], 1 + h))
    x_mine = xown[...].reshape(tokens, feat_in)
    w_in_load.wait()
    hidden = mm(x_mine, w_in[...])
    w_copy.wait_recv()
    for copy in x_copies:
        copy.wait_recv()
    hidden = hidden + mm(xoth[...].reshape(tokens, feat_in), woth[...])
    hidden = hidden.reshape(n, hops, per, width) + hop_embed[...].reshape(1, hops, 1, width)
    hidden = hidden.reshape(tokens, width)
    inv_root = lax.rsqrt(jnp.mean(hidden * hidden, axis=-1, keepdims=True) + EPS)
    normed = hidden * inv_root
    normed_s[...] = normed
    attn_in = (normed * gain[...]).astype(bf16)
    for copy in w_qkv_loads:
        copy.wait()
    proj_s[...] = mm(attn_in, w_qkv[...]).astype(bf16).reshape(n, hops, per, 3 * half)

    for copy in c_copies:
        copy.wait_recv()
    cot_copy = feat_copy(cot2.at[side], cot2.at[side], 5)

    row_head = lax.broadcasted_iota(jnp.int32, (half, half), 0) // HD
    col_head = lax.broadcasted_iota(jnp.int32, (half, half), 1) // HD
    ones = jnp.where(row_head == col_head, 1.0, 0.0).astype(bf16)
    scale = 1.0 / math.sqrt(HD)
    step = 2
    rows = step * per

    def part(ref, block, i, lo):
        return ref[block, i, :, lo * half : (lo + 1) * half].reshape(rows, half).astype(f32)

    def head_sums(pairs):
        total = mm(jnp.concatenate(pairs, axis=0).astype(bf16), ones)
        return [total[j * rows : (j + 1) * rows] for j in range(hops)]

    @pl.loop(0, n // step)
    def _(s):
        block = pl.ds(s * step, step)
        k = [part(proj_s, block, i, 1) for i in range(hops)]
        v = [part(proj_s, block, i, 2) for i in range(hops)]
        for i in range(hops):
            q = part(proj_s, block, i, 0)
            e = [jnp.exp(t * scale) for t in head_sums([q * k[j] for j in range(hops)])]
            inverse = 1.0 / sum(e)
            p = [t * inverse for t in e]
            mixed = sum(p[j].astype(bf16).astype(f32) * v[j] for j in range(hops))
            mixed_s[block, i] = mixed.astype(bf16).reshape(step, per, half)
            for j in range(hops):
                p_s[block, i * hops + j] = p[j].reshape(step, per, half)

    cot_copy.wait_recv()
    upstream = jnp.concatenate([cot2[0].reshape(tokens, half), cot2[1].reshape(tokens, half)], axis=1)

    kinds = ((1, 0, 2), (0,), (0,), (1, 0, 2), (1, 0, 2), (0,))
    s_out, s_q, s_k, s_v, s_ext, s_in = all_s = [
        (DirectScatter if bits == (0,) else Scatter)(
            bits, rest[6 * k], rest[6 * k + 1 : 6 * k + 6], rs_send.at[k], rs_recv.at[k], me
        )
        for k, bits in enumerate(kinds)
    ]

    def put(which, lo, value):
        ref = which.block
        ref[..., lo : lo + value.shape[1]] = value.astype(bf16).reshape(
            ref.shape[:-1] + (value.shape[1],)
        )

    put(s_out, 0, mm(upstream, mixed_s[...].reshape(tokens, half), TN))
    s_out.start(0)
    w_out_load.wait()
    gm_s[...] = mm(upstream, w_out[...], NT).astype(bf16).reshape(n, hops, per, half)

    @pl.loop(0, n // step)
    def _(s):
        block = pl.ds(s * step, step)
        k = [part(proj_s, block, i, 1) for i in range(hops)]
        v = [part(proj_s, block, i, 2) for i in range(hops)]
        grad_k = [0.0] * hops
        grad_v = [0.0] * hops
        for i in range(hops):
            q = part(proj_s, block, i, 0)
            g = part(gm_s, block, i, 0)
            p = [p_s[block, i * hops + j].reshape(rows, half) for j in range(hops)]
            gp = head_sums([g * v[j] for j in range(hops)])
            mean = sum(p[j] * gp[j] for j in range(hops))
            gs = [p[j] * (gp[j] - mean) * scale for j in range(hops)]
            grad_q = sum(gs[j] * k[j] for j in range(hops))
            for j in range(hops):
                grad_k[j] = grad_k[j] + gs[j] * q
                grad_v[j] = grad_v[j] + p[j].astype(bf16).astype(f32) * g
            gproj_s[block, i, :, 0:half] = grad_q.astype(bf16).reshape(step, per, half)
        for j in range(hops):
            gproj_s[block, j, :, half : 2 * half] = grad_k[j].astype(bf16).reshape(step, per, half)
            gproj_s[block, j, :, 2 * half :] = grad_v[j].astype(bf16).reshape(step, per, half)

    grad_proj = gproj_s[...].reshape(tokens, 3 * half)
    for c, which in enumerate((s_q, s_k, s_v)):
        put(which, 0, mm(attn_in, grad_proj[:, c * half : (c + 1) * half], TN))
        which.start(0)
    pown[...] = mm(grad_proj, w_qkv[...], NT).astype(bf16)
    p_copy = feat_copy(pown, poth, 6)

    p_copy.wait_recv()
    grad_attn = pown[...].astype(f32) + poth[...].astype(f32)
    normed = normed_s[...]
    grad_norm = grad_attn * gain[...]
    grad_hidden = upstream.astype(f32) + inv_root * (
        grad_norm - normed * jnp.mean(grad_norm * normed, axis=-1, keepdims=True)
    )
    grad_low = grad_hidden.astype(bf16)
    gain_low = (grad_attn * normed).astype(bf16)
    lanes = lax.broadcasted_iota(jnp.int32, (tokens, 128), 1)
    hop_of = (lax.broadcasted_iota(jnp.int32, (tokens, 128), 0) // per) % hops
    hop_hot = jnp.where(lanes == hop_of, 1.0, 0.0).astype(bf16)
    gain_hot = jnp.where(lanes == hops, 1.0, 0.0).astype(bf16)
    cut = feat_in - 128
    put(s_ext, 0, mm(grad_low, x_mine[:, cut:], TN))
    put(s_ext, 128, mm(grad_low, hop_hot, TN) + mm(gain_low, gain_hot, TN))
    s_ext.start(0)
    put(s_in, 0, mm(grad_low, x_mine[:, 0:cut], TN))
    s_in.start(0)

    for stage in range(2):
        for s in all_s:
            s.finish(stage)
            s.start(stage + 1)
    for s, result in zip(all_s, (o_out, o_q, o_k, o_v, o_ext, o_in)):
        result[...] = s.finish(2)
    for s in all_s:
        s.drain()
    for copy in id_copies + c_copies + x_copies + [w_copy, cot_copy, p_copy]:
        copy.wait_send()


def lay_out(hops, feat_in, bq, bk, bv, bout, bin_, bext, qkv, out, grad_in, grad_hop, grad_gain):
    cut = feat_in - 128
    qkv[0] = bq[...]
    qkv[1] = bk[...]
    qkv[2] = bv[...]
    out[...] = bout[...]
    grad_in[:, 0:cut] = bin_[...]
    grad_in[:, cut:] = bext[:, 0:128]
    turned = bext[:, 128:].T
    grad_hop[...] = turned[0:hops]
    grad_gain[...] = turned[hops : hops + 1]


def fused(node_ids, hop_table, w_in, hop_embed, norm_gain, w_qkv, w_out, cotangent):
    f32, bf16 = jnp.float32, jnp.bfloat16
    n = lax.axis_size("dp")
    nodes = node_ids.shape[0]
    per = nodes // n
    table_rows, hops, feat_in = hop_table.shape
    width = w_in.shape[1]
    half = w_out.shape[0]
    tokens = nodes * hops
    share = width // n
    dims = (n, per, hops, table_rows, feat_in, width, half)

    def vm(shape, kind=bf16):
        return pltpu.VMEM(shape, kind)

    def stages(columns):
        c = (share, columns)
        return [vm((2, 2, 2) + c), vm((2, 2) + c), vm((2, 2) + c), vm((2,) + c), vm((2,) + c), vm(c)]

    dma = pltpu.SemaphoreType.DMA
    scratch = [
        vm((table_rows, hops, feat_in)), vm((feat_in, width)), vm((width, 3 * half)), vm((half, width)),
        vm((nodes, hops, width)), vm((hops, table_rows, feat_in)), vm((hops, nodes, width)),
        vm((n, per, nodes), jnp.int32), vm((n, per, nodes), jnp.int32),
        vm((n, hops, per, half)), vm((2, n, hops, per, half)),
        vm((n, hops, per, feat_in)), vm((n, hops, per, feat_in)), vm((feat_in, width)),
        vm((tokens, width)), vm((tokens, width)), vm((tokens, width), f32),
        vm((n, hops, per, 3 * half)), vm((n, hops, per, half)),
        vm((n, hops, per, 3 * half)), vm((n, hops, per, half)),
    ]
    scratch += [vm((n, hops * hops, per, half), f32)] + stages(half) * 4 + stages(256) + stages(feat_in - 128)
    scratch += [dma((7,)), dma((n,)), dma((n,)), dma((n,)), dma((n,)), dma((7,)), dma((7,)), dma((6, 4)), dma((6, 4))]
    vmem = pl.BlockSpec(memory_space=pltpu.VMEM)
    hbm = pl.BlockSpec(memory_space=pl.ANY)
    blocks = pl.pallas_call(
        functools.partial(kernel, dims),
        out_shape=tuple(
            jax.ShapeDtypeStruct((share, c), f32) for c in (half, half, half, half, feat_in - 128, 256)
        ),
        in_specs=[vmem, hbm, hbm, vmem, vmem, hbm, hbm, hbm],
        out_specs=(vmem,) * 6,
        scratch_shapes=scratch,
        compiler_params=pltpu.CompilerParams(
            collective_id=0, has_side_effects=True, vmem_limit_bytes=56 * 1024 * 1024
        ),
    )(
        node_ids.reshape(1, nodes), hop_table, w_in, hop_embed,
        norm_gain.reshape(1, width), w_qkv.transpose(1, 0, 2), w_out, cotangent,
    )
    qkv, out, grad_in, grad_hop, grad_gain = pl.pallas_call(
        functools.partial(lay_out, hops, feat_in),
        out_shape=(
            jax.ShapeDtypeStruct((3, share, half), f32),
            jax.ShapeDtypeStruct((share, half), f32),
            jax.ShapeDtypeStruct((share, feat_in), f32),
            jax.ShapeDtypeStruct((hops, share), f32),
            jax.ShapeDtypeStruct((1, share), f32),
        ),
        in_specs=[vmem] * 6,
        out_specs=(vmem,) * 5,
    )(*blocks)
    return grad_in.T, grad_hop, grad_gain.reshape(share), qkv.transpose(1, 0, 2), out.T


def solution(mesh):
    fits = mesh.shape["dp"] == 8 and mesh.shape["feat"] == 2
    placed = (
        P(("grp", "dp")),
        P(("grp", "dp"), None, "feat"),
        P("feat", None),
        P(),
        P(),
        P(None, None, "feat"),
        P("feat", None),
        P(("grp", "dp"), None, None),
    )
    return jax.shard_map(
        fused if fits else body,
        mesh=mesh,
        in_specs=placed,
        out_specs=(
            P(("grp", "feat"), "dp"),
            P("grp", "dp"),
            P(("grp", "dp")),
            P(("grp", "dp"), None, "feat"),
            P(("grp", "feat"), "dp"),
        ),
        check_vma=False,
    )
```

```python
import functools
import math

import jax
import jax.numpy as jnp
from jax import lax
from jax.experimental import pallas as pl
from jax.experimental.pallas import tpu as pltpu
from jax.sharding import PartitionSpec as P

HD = 64


EPS = 1e-06


def body(node_ids, hop_table, w_in, hop_embed, norm_gain, w_qkv, w_out, cotangent):
    f32 = jnp.float32
    bf16 = jnp.bfloat16
    dp_count = lax.axis_size("dp")
    table_rows = hop_table.shape[0]
    node_count = node_ids.shape[0]
    hop_count = hop_table.shape[1]
    width = w_in.shape[1]
    half_width = w_out.shape[0]
    head_local = half_width // HD
    token_count = node_count * hop_count
    scale = 1.0 / math.sqrt(HD)
    per_owner = node_count // dp_count
    owner_of = node_ids // table_rows
    sort_order = jnp.argsort(owner_of, stable=True)
    asked_rows = (node_ids[sort_order] % table_rows).reshape(dp_count, per_owner)
    found = hop_table[lax.all_to_all(asked_rows, "dp", split_axis=0, concat_axis=0, tiled=True)]
    fetched = lax.all_to_all(found, "dp", split_axis=0, concat_axis=0, tiled=True)
    flat_in = fetched.reshape(token_count, fetched.shape[-1])
    upstream = cotangent[sort_order].reshape(token_count, width)
    full_in, full_weight = (
        lax.all_gather(flat_in, "feat", axis=1, tiled=True),
        lax.all_gather(w_in, "feat", axis=0, tiled=True),
    )
    hidden = jnp.dot(full_in, full_weight, preferred_element_type=f32)
    hidden = (hidden.reshape(node_count, hop_count, width) + hop_embed[None]).reshape(
        token_count, width
    )
    mean_square = jnp.mean(hidden * hidden, axis=-1, keepdims=True)
    inv_root = lax.rsqrt(mean_square + EPS)
    normed = hidden * inv_root
    attn_in = (normed * norm_gain).astype(bf16)
    qkv_weight = w_qkv.reshape(width, 3 * half_width)
    projected = jnp.dot(attn_in, qkv_weight, preferred_element_type=f32).astype(bf16)
    projected = projected.reshape(node_count, hop_count, 3, head_local, HD)
    query = projected[:, :, 0]
    keys = projected[:, :, 1]
    values = projected[:, :, 2]
    scores = jnp.einsum("nihd,njhd->nhij", query, keys, preferred_element_type=f32) * scale
    probs = jnp.exp(scores)
    probs = probs / jnp.sum(probs, axis=-1, keepdims=True)
    probs_low = probs.astype(bf16)
    mixed = jnp.einsum("nhij,njhd->nihd", probs_low, values, preferred_element_type=f32).astype(
        bf16
    )
    mixed = mixed.reshape(token_count, half_width)
    grad_out = jnp.einsum("mc,me->ce", mixed, upstream, preferred_element_type=f32)
    grad_mixed = jnp.einsum("me,ce->mc", upstream, w_out, preferred_element_type=f32).astype(bf16)
    grad_mixed = grad_mixed.reshape(node_count, hop_count, head_local, HD)
    grad_probs = jnp.einsum("nihd,njhd->nhij", grad_mixed, values, preferred_element_type=f32)
    grad_values = jnp.einsum("nhij,nihd->njhd", probs_low, grad_mixed, preferred_element_type=f32)
    grad_scores = probs * (grad_probs - jnp.sum(probs * grad_probs, axis=-1, keepdims=True)) * scale
    grad_query = jnp.einsum("nhij,njhd->nihd", grad_scores, keys.astype(f32))
    grad_keys = jnp.einsum("nhij,nihd->njhd", grad_scores, query.astype(f32))
    grad_proj = jnp.stack([grad_query, grad_keys, grad_values], axis=2).astype(bf16)
    grad_proj = grad_proj.reshape(token_count, 3 * half_width)
    grad_qkv = jnp.einsum("mc,me->ce", attn_in, grad_proj, preferred_element_type=f32).reshape(
        width, 3, half_width
    )
    partial_attn = jnp.einsum(
        "me,ce->mc", grad_proj, qkv_weight, preferred_element_type=f32
    ).astype(bf16)
    grad_attn = lax.psum(partial_attn, "feat").astype(jnp.float32)
    grad_gain = jnp.sum(grad_attn * normed, axis=0)
    grad_normed = grad_attn * norm_gain
    grad_hidden = upstream.astype(f32) + inv_root * (
        grad_normed - normed * jnp.mean(grad_normed * normed, axis=-1, keepdims=True)
    )
    grad_hop = jnp.sum(grad_hidden.reshape(node_count, hop_count, width), axis=0)
    grad_in = jnp.einsum("mc,me->ce", flat_in, grad_hidden.astype(bf16), preferred_element_type=f32)
    summed = (
        lax.psum_scatter(grad_in, "dp", scatter_dimension=1, tiled=True),
        lax.psum_scatter(grad_hop, "dp", scatter_dimension=1, tiled=True),
        lax.psum_scatter(grad_gain, "dp", scatter_dimension=0, tiled=True),
        lax.psum_scatter(grad_qkv, "dp", scatter_dimension=0, tiled=True),
        lax.psum_scatter(grad_out, "dp", scatter_dimension=1, tiled=True),
    )
    return (summed[0], summed[1], summed[2], summed[3], summed[4])


MESH = pl.DeviceIdType.MESH
NT = (((1,), (1,)), ((), ()))
TN = (((0,), (0,)), ((), ()))


def mm(a, b, dims=(((1,), (0,)), ((), ()))):
    return lax.dot_general(a, b, dims, preferred_element_type=jnp.float32)


class Scatter:
    def __init__(self, bits, block, bufs, send_sem, recv_sem, me):
        self.bits, self.block, self.bufs, self.me = bits, block, bufs, me
        self.send_sem, self.recv_sem = send_sem, recv_sem
        self.copies = []

    def bit(self, which):
        return (self.me // (1 << which)) % 2

    def pick(self, stage, side):
        ref = self.block if stage == 0 else self.bufs[2 * stage - 1]
        left = [b for b in (2, 1, 0) if b not in self.bits[:stage]]
        axis = left.index(self.bits[stage])
        index = tuple([slice(None)] * axis + [side])
        return ref.at[index]

    def start(self, stage):
        which = self.bits[stage]
        mine = self.bit(which)
        peer = self.me + (1 - 2 * mine) * (1 << which)
        copy = pltpu.make_async_remote_copy(
            src_ref=self.pick(stage, 1 - mine),
            dst_ref=self.bufs[2 * stage],
            send_sem=self.send_sem.at[stage],
            recv_sem=self.recv_sem.at[stage],
            device_id={"dp": peer},
            device_id_type=MESH,
        )
        copy.start()
        self.copies.append(copy)

    def finish(self, stage):
        self.copies[stage].wait_recv()
        mine = self.bit(self.bits[stage])
        total = self.pick(stage, mine)[...].astype(jnp.float32) + self.bufs[2 * stage][...].astype(
            jnp.float32
        )
        if stage < 2:
            self.bufs[2 * stage + 1][...] = total.astype(jnp.bfloat16)
        return total

    def drain(self):
        for copy in self.copies:
            copy.wait_send()


class DirectScatter(Scatter):
    def block_of(self, r):
        high, low = self.bit(2), self.bit(1)
        return (1 - high if r & 2 else high), (1 - low if r & 1 else low)

    def start(self, stage):
        if stage == 0:
            super().start(0)
        if stage != 1:
            return
        for r in (1, 2, 3):
            high, low = self.block_of(r)
            copy = pltpu.make_async_remote_copy(
                src_ref=self.bufs[1].at[high, low],
                dst_ref=self.bufs[4] if r == 3 else self.bufs[2].at[r - 1],
                send_sem=self.send_sem.at[r],
                recv_sem=self.recv_sem.at[r],
                device_id={"dp": 4 * high + 2 * low + self.bit(0)},
                device_id_type=MESH,
            )
            copy.start()
            self.copies.append(copy)

    def finish(self, stage):
        if stage == 0:
            return super().finish(0)
        if stage == 1:
            return None
        for copy in self.copies[1:]:
            copy.wait_recv()
        high, low = self.block_of(0)
        total = self.bufs[1][high, low].astype(jnp.float32)
        for part in (self.bufs[2][0], self.bufs[2][1], self.bufs[4][...]):
            total = total + part.astype(jnp.float32)
        return total


def kernel(
    dims, ids, tab_hbm, w_in_hbm, hop_embed, gain, w_qkv_hbm, w_out_hbm, cot_hbm,
    o_q, o_k, o_v, o_out, o_in, o_in1, o_ext,
    tab_in, w_in, w_qkv, w_out, cot_in, tab, cot,
    asked, irecv, csend, cot2, xown, xoth, woth, pown, poth, normed_s, proj_s, gm_s, gproj_s, mixed_s,
    p_s, e_send, e_recv, attn_t, *rest,
):
    n, per, hops, table_rows, feat_in, width, half = dims
    in_sem, id_send, id_recv, c_send, c_recv, f_send, f_recv, rs_send, rs_recv, e_sem, e_got = rest[36:]
    f32, bf16 = jnp.float32, jnp.bfloat16
    nodes = n * per
    tokens = nodes * hops
    me = lax.axis_index("dp")
    side = lax.axis_index("feat")

    def peer_of(r):
        return lax.rem(me + r, n)

    loads = []

    def load(src, dst):
        copy = pltpu.make_async_copy(src, dst, in_sem.at[len(loads)])
        copy.start()
        loads.append(copy)
        return copy

    cot_load = load(cot_hbm, cot_in)
    tab_load = load(tab_hbm, tab_in)
    w_in_load = load(w_in_hbm, w_in)
    w_qkv_loads = [
        load(w_qkv_hbm.at[c], w_qkv.at[:, c * half : (c + 1) * half]) for c in range(3)
    ]
    w_out_load = load(w_out_hbm, w_out)

    barrier = pltpu.get_barrier_semaphore()
    for r in range(1, n):
        pl.semaphore_signal(barrier, inc=1, device_id={"dp": peer_of(r)}, device_id_type=MESH)
    pl.semaphore_signal(barrier, inc=1, device_id={"feat": 1 - side}, device_id_type=MESH)

    ids_f = ids[...].astype(f32)
    owner = jnp.floor((ids_f + 0.5) * (1.0 / table_rows))
    local = ids_f - owner * table_rows
    rows_i = lax.broadcasted_iota(jnp.int32, (nodes, nodes), 0)
    cols_i = lax.broadcasted_iota(jnp.int32, (nodes, nodes), 1)
    wide = jnp.broadcast_to(owner, (nodes, nodes))
    same = jnp.where((wide.T == wide) & (rows_i < cols_i), 1.0, 0.0)
    slot = owner * per + jnp.sum(same, axis=0, keepdims=True)
    place = jnp.where(slot == rows_i.astype(f32), 1.0, 0.0)
    wanted = jnp.sum(place * local, axis=1, keepdims=True)
    asked[...] = jnp.broadcast_to(wanted, (nodes, nodes)).astype(jnp.int32).reshape(n, per, nodes)
    irecv[pl.ds(me, 1)] = asked[pl.ds(me, 1)]

    pl.semaphore_wait(barrier, n)

    def feat_copy(src, dst, k):
        copy = pltpu.make_async_remote_copy(
            src_ref=src, dst_ref=dst, send_sem=f_send.at[k], recv_sem=f_recv.at[k],
            device_id={"feat": 1 - side}, device_id_type=MESH,
        )
        copy.start()
        return copy

    id_copies = []
    for r in range(1, n):
        copy = pltpu.make_async_remote_copy(
            src_ref=asked.at[peer_of(r)], dst_ref=irecv.at[me],
            send_sem=id_send.at[r], recv_sem=id_recv.at[r],
            device_id={"dp": peer_of(r)}, device_id_type=MESH,
        )
        copy.start()
        id_copies.append(copy)
    w_copy = feat_copy(w_in_hbm, woth, 0)
    cot_load.wait()
    cot[...] = jnp.swapaxes(cot_in[...], 0, 1)

    place_low = place.astype(bf16)
    for h in range(hops):
        csend[:, h] = mm(place_low, cot[h, :, pl.ds(pl.multiple_of(side * half, half), half)]).astype(bf16).reshape(n, per, half)
    cot2[side, pl.ds(me, 1)] = csend[pl.ds(me, 1)]
    c_copies = []
    for r in range(1, n):
        copy = pltpu.make_async_remote_copy(
            src_ref=csend.at[peer_of(r)], dst_ref=cot2.at[side, me],
            send_sem=c_send.at[r], recv_sem=c_recv.at[r],
            device_id={"dp": peer_of(r)}, device_id_type=MESH,
        )
        copy.start()
        c_copies.append(copy)

    tab_load.wait()
    tab[...] = jnp.swapaxes(tab_in[...], 0, 1)
    for copy in id_copies:
        copy.wait_recv()
    got = irecv[...].reshape(nodes, nodes)
    spans = table_rows // nodes
    hot = jnp.concatenate(
        [jnp.where(got == cols_i + nodes * b, 1.0, 0.0).astype(bf16) for b in range(spans)], axis=1
    )
    x_copies = []
    for h in range(hops):
        xown[:, h] = mm(hot, tab[h]).astype(bf16).reshape(n, per, feat_in)
        x_copies.append(feat_copy(xown.at[:, h], xoth.at[:, h], 1 + h))
    x_mine = xown[...].reshape(tokens, feat_in)
    w_in_load.wait()
    hidden = mm(x_mine, w_in[...])
    w_copy.wait_recv()
    for copy in x_copies:
        copy.wait_recv()
    hidden = hidden + mm(xoth[...].reshape(tokens, feat_in), woth[...])
    hidden = hidden.reshape(n, hops, per, width) + hop_embed[...].reshape(1, hops, 1, width)
    hidden = hidden.reshape(tokens, width)
    inv_root = lax.rsqrt(jnp.mean(hidden * hidden, axis=-1, keepdims=True) + EPS)
    normed = hidden * inv_root
    normed_s[...] = normed
    attn_in = (normed * gain[...]).astype(bf16)
    attn_t[...] = attn_in.T
    for copy in w_qkv_loads:
        copy.wait()
    proj_s[...] = mm(attn_in, w_qkv[...]).astype(bf16).reshape(n, hops, per, 3 * half)

    for copy in c_copies:
        copy.wait_recv()
    cot_copy = feat_copy(cot2.at[side], cot2.at[side], 5)

    row_head = lax.broadcasted_iota(jnp.int32, (half, half), 0) // HD
    col_head = lax.broadcasted_iota(jnp.int32, (half, half), 1) // HD
    ones = jnp.where(row_head == col_head, 1.0, 0.0).astype(bf16)
    scale = 1.0 / math.sqrt(HD)
    step = 2
    rows = step * per

    def part(ref, block, i, lo):
        return ref[block, i, :, lo * half : (lo + 1) * half].reshape(rows, half).astype(f32)

    def head_sums(pairs):
        total = mm(jnp.concatenate(pairs, axis=0).astype(bf16), ones)
        return [total[j * rows : (j + 1) * rows] for j in range(hops)]

    @pl.loop(0, n // step)
    def _(s):
        block = pl.ds(s * step, step)
        k = [part(proj_s, block, i, 1) for i in range(hops)]
        v = [part(proj_s, block, i, 2) for i in range(hops)]
        for i in range(hops):
            q = part(proj_s, block, i, 0)
            e = [jnp.exp(t * scale) for t in head_sums([q * k[j] for j in range(hops)])]
            inverse = 1.0 / sum(e)
            p = [t * inverse for t in e]
            mixed = sum(p[j].astype(bf16).astype(f32) * v[j] for j in range(hops))
            mixed_s[block, i] = mixed.astype(bf16).reshape(step, per, half)
            for j in range(hops):
                p_s[block, i * hops + j] = p[j].reshape(step, per, half)

    cot_copy.wait_recv()
    upstream = jnp.concatenate([cot2[0].reshape(tokens, half), cot2[1].reshape(tokens, half)], axis=1)

    kinds = ((1, 0, 2), (0,), (0,), (1, 0, 2), (1, 0, 2), (1, 0, 2))
    s_out, s_q, s_k, s_v, s_ext, s_in = all_s = [
        (DirectScatter if bits == (0,) else Scatter)(
            bits, rest[6 * k], rest[6 * k + 1 : 6 * k + 6], rs_send.at[k], rs_recv.at[k], me
        )
        for k, bits in enumerate(kinds)
    ]

    def put(which, lo, value):
        ref = which.block
        ref[..., lo : lo + value.shape[1]] = value.astype(bf16).reshape(
            ref.shape[:-1] + (value.shape[1],)
        )

    put(s_out, 0, mm(upstream, mixed_s[...].reshape(tokens, half), TN))
    s_out.start(0)
    w_out_load.wait()
    gm_s[...] = mm(upstream, w_out[...], NT).astype(bf16).reshape(n, hops, per, half)

    @pl.loop(0, n // step)
    def _(s):
        block = pl.ds(s * step, step)
        k = [part(proj_s, block, i, 1) for i in range(hops)]
        v = [part(proj_s, block, i, 2) for i in range(hops)]
        grad_k = [0.0] * hops
        grad_v = [0.0] * hops
        for i in range(hops):
            q = part(proj_s, block, i, 0)
            g = part(gm_s, block, i, 0)
            p = [p_s[block, i * hops + j].reshape(rows, half) for j in range(hops)]
            gp = head_sums([g * v[j] for j in range(hops)])
            mean = sum(p[j] * gp[j] for j in range(hops))
            gs = [p[j] * (gp[j] - mean) * scale for j in range(hops)]
            grad_q = sum(gs[j] * k[j] for j in range(hops))
            for j in range(hops):
                grad_k[j] = grad_k[j] + gs[j] * q
                grad_v[j] = grad_v[j] + p[j].astype(bf16).astype(f32) * g
            gproj_s[block, i, :, 0:half] = grad_q.astype(bf16).reshape(step, per, half)
        for j in range(hops):
            gproj_s[block, j, :, half : 2 * half] = grad_k[j].astype(bf16).reshape(step, per, half)
            gproj_s[block, j, :, 2 * half :] = grad_v[j].astype(bf16).reshape(step, per, half)

    grad_proj = gproj_s[...].reshape(tokens, 3 * half)
    for c, which in enumerate((s_q, s_k, s_v)):
        put(which, 0, mm(attn_t[...], grad_proj[:, c * half : (c + 1) * half]))
        which.start(0)
    pown[...] = mm(grad_proj, w_qkv[...], NT).astype(bf16)
    p_copy = feat_copy(pown, poth, 6)

    p_copy.wait_recv()
    grad_attn = pown[...].astype(f32) + poth[...].astype(f32)
    normed = normed_s[...]
    grad_norm = grad_attn * gain[...]
    grad_hidden = upstream.astype(f32) + inv_root * (
        grad_norm - normed * jnp.mean(grad_norm * normed, axis=-1, keepdims=True)
    )
    grad_t = grad_hidden.astype(bf16).T
    cut = feat_in - 128
    put(s_ext, 0, mm(grad_t, x_mine[:, cut:]))
    s_ext.start(0)
    put(s_in, 0, mm(grad_t, x_mine[:, 0:cut]))
    s_in.start(0)
    hop_sum = jnp.sum(jnp.sum(grad_hidden.reshape(n, hops, per, width), axis=0), axis=1)
    gain_sum = jnp.sum(grad_attn * normed, axis=0, keepdims=True)
    share = width // n
    e_send[...] = jnp.zeros_like(e_send)
    for d in range(n):
        e_send[d, 0:hops, 0:share] = hop_sum[:, d * share : (d + 1) * share]
        e_send[d, hops : hops + 1, 0:share] = gain_sum[:, d * share : (d + 1) * share]
    e_recv[pl.ds(me, 1)] = e_send[pl.ds(me, 1)]
    e_copies = []
    for r in range(1, n):
        copy = pltpu.make_async_remote_copy(
            src_ref=e_send.at[peer_of(r)], dst_ref=e_recv.at[me],
            send_sem=e_sem.at[r], recv_sem=e_got.at[r],
            device_id={"dp": peer_of(r)}, device_id_type=MESH,
        )
        copy.start()
        e_copies.append(copy)

    for stage in range(2):
        for s in all_s:
            s.finish(stage)
            s.start(stage + 1)
    for s, result in zip(all_s, (o_out, o_q, o_k, o_v, o_in1, o_in)):
        result[...] = s.finish(2)
    for copy in e_copies:
        copy.wait_recv()
    o_ext[...] = jnp.sum(e_recv[...], axis=0)
    for s in all_s:
        s.drain()
    for copy in id_copies + c_copies + x_copies + e_copies + [w_copy, cot_copy, p_copy]:
        copy.wait_send()


def lay_out(hops, feat_in, bq, bk, bv, bout, bin_, bin1, bext, qkv, out, grad_in, grad_hop, grad_gain):
    cut = feat_in - 128
    qkv[0] = bq[...]
    qkv[1] = bk[...]
    qkv[2] = bv[...]
    out[...] = bout[...]
    grad_in[:, 0:cut] = bin_[...]
    grad_in[:, cut:] = bin1[...]
    share = grad_hop.shape[1]
    grad_hop[...] = bext[0:hops, 0:share]
    grad_gain[...] = bext[hops : hops + 1, 0:share]


def fused(node_ids, hop_table, w_in, hop_embed, norm_gain, w_qkv, w_out, cotangent):
    f32, bf16 = jnp.float32, jnp.bfloat16
    n = lax.axis_size("dp")
    nodes = node_ids.shape[0]
    per = nodes // n
    table_rows, hops, feat_in = hop_table.shape
    width = w_in.shape[1]
    half = w_out.shape[0]
    tokens = nodes * hops
    share = width // n
    dims = (n, per, hops, table_rows, feat_in, width, half)

    def vm(shape, kind=bf16):
        return pltpu.VMEM(shape, kind)

    def stages(columns):
        c = (share, columns)
        return [vm((2, 2, 2) + c), vm((2, 2) + c), vm((2, 2) + c), vm((2,) + c), vm((2,) + c), vm(c)]

    dma = pltpu.SemaphoreType.DMA
    scratch = [
        vm((table_rows, hops, feat_in)), vm((feat_in, width)), vm((width, 3 * half)), vm((half, width)),
        vm((nodes, hops, width)), vm((hops, table_rows, feat_in)), vm((hops, nodes, width)),
        vm((n, per, nodes), jnp.int32), vm((n, per, nodes), jnp.int32),
        vm((n, hops, per, half)), vm((2, n, hops, per, half)),
        vm((n, hops, per, feat_in)), vm((n, hops, per, feat_in)), vm((feat_in, width)),
        vm((tokens, width)), vm((tokens, width)), vm((tokens, width), f32),
        vm((n, hops, per, 3 * half)), vm((n, hops, per, half)),
        vm((n, hops, per, 3 * half)), vm((n, hops, per, half)),
    ]
    scratch += [vm((n, hops * hops, per, half), f32), vm((n, 8, 128), f32), vm((n, 8, 128), f32), vm((width, tokens))] + stages(half) * 4 + stages(128) + stages(feat_in - 128)
    scratch += [dma((7,)), dma((n,)), dma((n,)), dma((n,)), dma((n,)), dma((7,)), dma((7,)), dma((6, 4)), dma((6, 4)), dma((n,)), dma((n,))]
    vmem = pl.BlockSpec(memory_space=pltpu.VMEM)
    hbm = pl.BlockSpec(memory_space=pl.ANY)
    blocks = pl.pallas_call(
        functools.partial(kernel, dims),
        out_shape=tuple(
            jax.ShapeDtypeStruct((share, c), f32) for c in (half, half, half, half, feat_in - 128, 128)
        )
        + (jax.ShapeDtypeStruct((8, 128), f32),),
        in_specs=[vmem, hbm, hbm, vmem, vmem, hbm, hbm, hbm],
        out_specs=(vmem,) * 7,
        scratch_shapes=scratch,
        compiler_params=pltpu.CompilerParams(
            collective_id=0, has_side_effects=True, vmem_limit_bytes=56 * 1024 * 1024
        ),
    )(
        node_ids.reshape(1, nodes), hop_table, w_in, hop_embed,
        norm_gain.reshape(1, width), w_qkv.transpose(1, 0, 2), w_out, cotangent,
    )
    qkv, out, grad_in, grad_hop, grad_gain = pl.pallas_call(
        functools.partial(lay_out, hops, feat_in),
        out_shape=(
            jax.ShapeDtypeStruct((3, share, half), f32),
            jax.ShapeDtypeStruct((share, half), f32),
            jax.ShapeDtypeStruct((share, feat_in), f32),
            jax.ShapeDtypeStruct((hops, share), f32),
            jax.ShapeDtypeStruct((1, share), f32),
        ),
        in_specs=[vmem] * 7,
        out_specs=(vmem,) * 5,
    )(*blocks)
    return grad_in.T, grad_hop, grad_gain.reshape(share), qkv.transpose(1, 0, 2), out.T


def solution(mesh):
    fits = mesh.shape["dp"] == 8 and mesh.shape["feat"] == 2
    placed = (
        P(("grp", "dp")),
        P(("grp", "dp"), None, "feat"),
        P("feat", None),
        P(),
        P(),
        P(None, None, "feat"),
        P("feat", None),
        P(("grp", "dp"), None, None),
    )
    return jax.shard_map(
        fused if fits else body,
        mesh=mesh,
        in_specs=placed,
        out_specs=(
            P(("grp", "feat"), "dp"),
            P("grp", "dp"),
            P(("grp", "dp")),
            P(("grp", "dp"), None, "feat"),
            P(("grp", "feat"), "dp"),
        ),
        check_vma=False,
    )
```
